512 devices in a mesh: obs: 64 (over z, x), mem: 8 (over y, core).
Axes of the slice: x: 4, y: 4, z: 16, core: 2. Of those that a mesh axis runs over, the one named last changes fastest.
Arguments:
- anomalies: bfloat16 [256, 131072], P('mem', 'obs'), may hold values from -4 to 4
- innovations: float32 [256, 131072], P('mem', 'obs'), may hold values from -108 to 108
- obs_error: float32 [131072], P('obs'), may hold values from 1 to 4
- positions: bfloat16 [2, 131072], P(None, 'obs'), may hold values from 0 to 16, as said below
- pair_far: int32 [256], P('obs'), may hold values from 0 to 1, as said below
Outputs:
- solution: float32 [256, 131072], P('mem', 'obs')
- residual: float32 [256, 131072], P('mem', 'obs')
The draws below stay inside these ranges and needn't reach their ends.
Inputs may be any that keep to these rules, and one draw needn't show every extreme that they name: pair_far[a] is 1 when the block pair (a, a + 2) is listed and 0 otherwise; it is 0 for the last two blocks. positions[0, n] lies in [0, 1]; positions[1, n] lies in [0, 16].
All inputs are finite; a program needn't handle non-finite values.
Results may differ from the reference program's by a relative error of at most 0.0003.
Values may be sent and summed in bfloat16 or wider, within the bound.
A program may use at most 64 MiB of HBM per device.

```python
import math
import jax
import jax.numpy as jnp
from jax import lax

B = 512
BPD = 4
ITERS = 2
MEMBERS = 256
NB = 256
NOBS = 131072


def draw_anomalies(key, part):
    key = jax.random.fold_in(key, 11)
    values = jnp.clip(jax.random.normal(key, (MEMBERS, NOBS), jnp.float32), -4.0, 4.0)
    return values.astype(jnp.bfloat16)


def draw_innovations(key, part):
    key = jax.random.fold_in(key, 12)
    key_member, key_obs, key_base = jax.random.split(key, 3)
    member_scale = jnp.exp(jax.random.uniform(key_member, (MEMBERS, 1), jnp.float32, -1.2039728, 1.0986123))
    obs_scale = jnp.exp(jax.random.uniform(key_obs, (1, NOBS), jnp.float32, -1.2039728, 1.0986123))
    fraction = jnp.arange(NOBS, dtype=jnp.float32) / NOBS
    base = jnp.clip(jax.random.normal(key_base, (MEMBERS, NOBS), jnp.float32), -4.0, 4.0)
    values = base * (1.0 + 2.0 * fraction)[None, :]
    return (values * member_scale * obs_scale).astype(jnp.float32)


def draw_positions(key, part):
    key = jax.random.fold_in(key, 13)
    key_along, key_across = jax.random.split(key, 2)
    along = jax.random.uniform(key_along, (NOBS,), jnp.float32)
    across = jax.random.uniform(key_across, (NOBS,), jnp.float32)
    return jnp.stack([along, across * (B // 32)], axis=0).astype(jnp.bfloat16)


def draw_pair_far(key, part):
    key = jax.random.fold_in(key, 14)
    key_level, key_coin = jax.random.split(key, 2)
    level = jax.random.randint(key_level, (NB // BPD,), 0, 5)
    spread = jnp.repeat(level, BPD, total_repeat_length=NB)
    coin = jax.random.randint(key_coin, (NB,), 0, 4)
    listed = (coin < spread).astype(jnp.int32)
    return jnp.where(jnp.arange(NB) < NB - 2, listed, 0).astype(jnp.int32)


def block_scale(rng, dims, shards, low, top_value):
    level, own = 1.0, jax.random.fold_in(rng, 6)
    for dim, blocks in shards:
        heights = jnp.exp(jax.random.uniform(jax.random.fold_in(own, dim), (blocks,), jnp.float32, low / len(shards), top_value / len(shards)))
        level = level * jnp.repeat(heights, dims[dim] // blocks).reshape([-1 if axis == dim else 1 for axis in range(len(dims))])
    return level


def setup_inputs(seed: int = 0) -> dict:
    splits = jax.random.split(jax.random.key(seed), 6)
    return {
        "anomalies": draw_anomalies(jax.random.fold_in(splits[5], 71), 0),
        "innovations": draw_innovations(jax.random.fold_in(splits[5], 71), 0),
        "obs_error": jnp.clip(jnp.exp(math.log(4.0) - 1.3862944 * jax.random.uniform(splits[2], (NOBS,), jnp.float32) ** block_scale(splits[2], (NOBS,), ((0, 64),), -0.2, 0.2)), 1.0, 4.0),
        "positions": draw_positions(jax.random.fold_in(splits[5], 71), 0),
        "pair_far": draw_pair_far(jax.random.fold_in(splits[5], 71), 0),
    }


epsilon = 1e-06
precise = lax.Precision.HIGHEST

def gaspari(distance):
    inner_part = (((-0.25 * distance + 0.5) * distance + 0.625) * distance - 5.0 / 3.0) * distance * distance + 1.0
    outer_arg = jnp.maximum(distance, 1.0)
    outer_part = ((((distance / 12.0 - 0.5) * distance + 0.625) * distance + 5.0 / 3.0) * distance - 5.0) * distance + 4.0 - 2.0 / (3.0 * outer_arg)
    return jnp.where(distance <= 1.0, inner_part, jnp.where(distance < 2.0, outer_part, 0.0))

def pair_taper(first_places, second_places, offset):
    first_places = first_places.astype(jnp.float32)
    second_places = second_places.astype(jnp.float32)
    along_gap = first_places[..., 0, :, None] - second_places[..., 0, None, :] - offset
    across = first_places[..., 1, :, None] - second_places[..., 1, None, :]
    return gaspari(jnp.sqrt(along_gap * along_gap + across * across))

def reference(anomalies, innovations, obs_error, positions, pair_far):
    members = anomalies.shape[0]
    inverse_count = 1.0 / (members - 1)
    ensemble = anomalies.reshape(members, NB, B).transpose(1, 0, 2)
    places = positions.reshape(2, NB, B).transpose(1, 0, 2)
    ensemble_pad = jnp.concatenate([ensemble, jnp.zeros((2, members, B), ensemble.dtype)], axis=0)
    places_pad = jnp.concatenate([places, jnp.zeros((2, 2, B), places.dtype)], axis=0)
    listed = [jnp.ones((NB,), jnp.float32), jnp.ones((NB,), jnp.float32), pair_far.astype(jnp.float32)]
    ensemble_wide = ensemble.astype(jnp.float32)
    couplings = []
    for offset in range(3):
        partner = ensemble_pad[offset:offset + NB].astype(jnp.float32)
        partner_places = places_pad[offset:offset + NB]
        raw_product = jnp.einsum('amx,amy->axy', ensemble_wide, partner, precision=precise)
        coupling = raw_product * inverse_count * pair_taper(places, partner_places, float(offset))
        couplings.append(coupling * listed[offset][:, None, None])

    def operate(vector):
        blocks = vector.reshape(members, NB, B).transpose(1, 0, 2)
        padded = jnp.concatenate([blocks, jnp.zeros((2, members, B), jnp.float32)], axis=0)
        result = jnp.zeros((NB + 2, members, B), jnp.float32)
        for offset in range(3):
            partner = padded[offset:offset + NB]
            result = result.at[:NB].add(jnp.einsum('axy,amy->amx', couplings[offset], partner, precision=precise))
            if offset > 0:
                result = result.at[offset:offset + NB].add(jnp.einsum('axy,amx->amy', couplings[offset], blocks, precision=precise))
        applied = result[:NB].transpose(1, 0, 2).reshape(members, NB * B)
        return applied + obs_error[None, :] * vector
    solution = jnp.zeros_like(innovations)
    residual = innovations
    direction = innovations
    norm_now = lax.optimization_barrier(jnp.sum(residual * residual, axis=1))
    for step_index in range(ITERS):
        operated = operate(direction)
        step_size = norm_now / lax.optimization_barrier(jnp.sum(direction * operated, axis=1))
        solution = solution + step_size[:, None] * direction
        residual = residual - step_size[:, None] * operated
        norm_next = lax.optimization_barrier(jnp.sum(residual * residual, axis=1))
        direction = residual + (norm_next / (norm_now + epsilon))[:, None] * direction
        norm_now = norm_next
    return (solution, residual)
```

```python
import functools
import math

import jax
import jax.numpy as jnp
from jax import lax
from jax.experimental import pallas as pl
from jax.experimental.pallas import tpu as pltpu
from jax.sharding import PartitionSpec as P

B = 512
NX = 4
EPSILON = 1e-06
ROOT2 = math.sqrt(2.0)
SCALE = 48.0 * ROOT2
MESH = pl.DeviceIdType.MESH
CHUNK = 16
PAIRS = [(0, 2), (0, 3), (1, 2), (1, 3), (0, 1), (1, 4), (0, 0), (0, 4), (1, 1), (1, 5)]
NT = (((1,), (1,)), ((), ()))


def remote(src, dst, send, recv, device):
    return pltpu.make_async_remote_copy(
        src_ref=src, dst_ref=dst, send_sem=send, recv_sem=recv, device_id=device, device_id_type=MESH
    )


def kernel(
    block, nobs, nmem, nx,
    anom, innov, oerr, places, far, x_out, r_out,
    X, XT, U, V, UH, CH, CL, TP, RAW, PI, META, SC, PP, W, W2, W3, COEF, R1A, R2A, R1B, R2B,
    a_send, a_recv, f_send, f_recv, u_send, u_recv, m_send, m_recv, v_send, v_recv, w_send, w_recv,
    r1_send, r1_recv, r2_send, r2_recv, q1_send, q1_recv, q2_send, q2_recv,
):
    f32, bf16 = jnp.float32, jnp.bfloat16
    half = 2 * block
    rows = anom.shape[0]
    rows2 = 2 * rows
    nz = nobs // nx
    o = lax.axis_index("obs")
    mm = lax.axis_index("mem")
    c = lax.rem(mm, 2)
    y2 = mm - c
    pm = y2 + 1 - c
    z = lax.div(o, nx)
    x = lax.rem(o, nx)
    left = (lax.rem(o + nobs - 1 + c, nobs), pm)
    right = (lax.rem(o + c, nobs), pm)
    partner = (o, pm)
    far_to = (lax.rem(o + nobs + 1 - 2 * c, nobs), mm)
    far_from = (lax.rem(o + nobs - 1 + 2 * c, nobs), mm)
    off_chip = (lax.rem(o + nobs - 1 + 2 * c, nobs), pm)
    i1 = x * 2 + c

    def peer1(d):
        idx = lax.rem(i1 + d, 2 * nx)
        return (z * nx + lax.div(idx, 2), y2 + lax.rem(idx, 2))

    def peer2(d):
        return (lax.rem(z + d, nz) * nx + x, mm)

    barrier = pltpu.get_barrier_semaphore()
    peers = [(o, lax.rem(mm + d, nmem)) for d in range(1, nmem)]
    peers += [left, right, far_to, far_from]
    peers += [peer1(d) for d in range(1, 2 * nx)]
    peers += [peer2(d) for d in range(1, nz)]
    for peer in peers:
        pl.semaphore_signal(barrier, inc=1, device_id=peer, device_id_type=MESH)

    own_rows = pl.ds(pl.multiple_of(mm * rows, rows), rows)
    core_rows = pl.ds(pl.multiple_of(c * rows, rows), rows)
    partner_rows = pl.ds(pl.multiple_of((1 - c) * rows, rows), rows)
    own_half = pl.ds(pl.multiple_of(c * half, half), half)
    other_half = pl.ds(pl.multiple_of((1 - c) * half, half), half)
    pf = places[...].astype(f32) * ROOT2
    for h in range(2):
        flags = jnp.concatenate(
            [jnp.full((1, block), far[2 * h + b].astype(f32), f32) for b in range(2)], axis=1
        )
        META[1 - c + h] = jnp.concatenate(
            [pf[:, h * half : (h + 1) * half], flags, jnp.zeros((5, half), f32)], axis=0
        )
    X[1, own_rows, :] = anom[:, own_half]
    pl.semaphore_wait(barrier, len(peers))

    meta_copy = remote(META.at[1], META.at[2 - 2 * c], m_send, m_recv, off_chip)
    meta_copy.start()
    meta_back = remote(META.at[1], META.at[2 * c], m_send, m_recv, off_chip)

    a_out, a_in = [], []
    for d in range(1, nmem):
        to = lax.rem(mm + d, nmem)
        source = lax.rem(mm + nmem - d, nmem)
        to_half = pl.ds(pl.multiple_of(lax.rem(to, 2) * half, half), half)
        copy = remote(anom.at[:, to_half], X.at[1, own_rows, :], a_send.at[d], a_recv.at[d], (o, to))
        copy.start()
        a_out.append(copy)
        src_rows = pl.ds(pl.multiple_of(source * rows, rows), rows)
        a_in.append(remote(anom.at[:, own_half], X.at[1, src_rows, :], a_send.at[d], a_recv.at[d], (o, to)))

    def forward(d):
        source = lax.rem(mm + nmem - d, nmem)
        piece = pl.ds(pl.multiple_of(source * rows, rows), rows)
        if d > 0:
            a_in[d - 1].wait_recv()
        one = remote(X.at[1, piece, :], X.at[2, piece, :], f_send.at[0, d], f_recv.at[0, d], left)
        two = remote(X.at[1, piece, :], X.at[0, piece, :], f_send.at[1, d], f_recv.at[1, d], right)
        one.start()
        two.start()
        return [one, two]

    def forwarded(slot, d):
        source = lax.rem(pm + nmem - d, nmem)
        piece = pl.ds(pl.multiple_of(source * rows, rows), rows)
        way = 0 if slot == 2 else 1
        device = left if slot == 2 else right
        return remote(X.at[1, piece, :], X.at[slot, piece, :], f_send.at[way, d], f_recv.at[way, d], device)

    f_out = forward(0)

    u_out = [
        remote(innov.at[:, own_half], U.at[2, core_rows, :], u_send.at[0], u_recv.at[0], left),
        remote(innov.at[:, own_half], U.at[0, core_rows, :], u_send.at[1], u_recv.at[1], right),
        remote(innov.at[:, other_half], U.at[1, core_rows, :], u_send.at[2], u_recv.at[2], partner),
        remote(innov.at[:, other_half], U.at[2 * c, core_rows, :], u_send.at[3], u_recv.at[3], far_to),
    ]
    u_in = [
        remote(innov.at[:, own_half], U.at[2, partner_rows, :], u_send.at[0], u_recv.at[0], left),
        remote(innov.at[:, own_half], U.at[0, partner_rows, :], u_send.at[1], u_recv.at[1], right),
        remote(innov.at[:, other_half], U.at[1, partner_rows, :], u_send.at[2], u_recv.at[2], partner),
        remote(innov.at[:, other_half], U.at[2 * c, core_rows, :], u_send.at[3], u_recv.at[3], far_to),
    ]
    for copy in u_out:
        copy.start()
    for h in range(2):
        U[1 - c + h, core_rows, :] = innov[:, h * half : (h + 1) * half]

    lanes = 128
    for k in range(half // lanes):
        for axis in range(2):
            line = META[1, axis : axis + 1, k * lanes : (k + 1) * lanes]
            PI[axis, k * lanes : (k + 1) * lanes, :] = jnp.broadcast_to(line, (lanes, lanes)).T

    def window(w):
        slot, part = divmod(w, 2)
        return slot, slice(part * block, (part + 1) * block)

    def taper(p):
        s, w = PAIRS[p]
        offset = w - 2 - s
        slot, cols = window(w)
        along = META[slot, 0:1, cols] + offset * ROOT2
        across = META[slot, 1:2, cols]
        near = abs(offset) < 2

        def step(k, carry):
            at = pl.multiple_of(k * CHUNK, CHUNK)
            mine = pl.ds(s * block + at, CHUNK)
            g = jnp.concatenate([PI[0, mine, :]] * (block // lanes), axis=1) - along
            h = jnp.concatenate([PI[1, mine, :]] * (block // lanes), axis=1) - across
            square = g * g + h * h
            if near:
                square = jnp.maximum(square, 1e-30)
            inverse = lax.rsqrt(square)
            y = square * inverse
            rest = jnp.maximum(2.0 * ROOT2 - y, 0.0)
            rest = rest * rest
            value = (rest * rest) * ((y - inverse) + 2.0 * ROOT2)
            if near:
                inner = (-3.0 * y + 0.125 * SCALE) * y + 0.3125 * SCALE / ROOT2
                inner = (inner * y - (5.0 / 6.0) * SCALE) * square + SCALE
                value = jnp.maximum(value, inner)
            TP[p, pl.ds(at, CHUNK), :] = value
            return carry

        lax.fori_loop(0, block // CHUNK, step, 0, unroll=2)

    for p in range(4):
        taper(p)
        if p == 0:
            f_out += forward(1)
        else:
            f_out += forward(2 * p) + forward(2 * p + 1) if 2 * p + 1 < nmem else []
    meta_back.wait_recv()
    for p in range(4, 10):
        taper(p)

    q = 2 * o + c
    first = jnp.where(q > 0, 1.0, 0.0).astype(f32)
    last = jnp.where(q < 2 * nobs - 1, 1.0, 0.0).astype(f32)
    factor = 1.0 / (SCALE * (rows * nmem - 1))
    for p, (s, w) in enumerate(PAIRS):
        offset = w - 2 - s
        line = jnp.full((1, block), factor, f32)
        if w < 2:
            line = line * first
        if w > 3:
            line = line * last
        if offset == 2:
            line = line * META[1, 2:3, s * block : (s + 1) * block]
        if offset == -2:
            line = line * META[0, 2:3, s * block : (s + 1) * block]
        SC[p : p + 1, :] = line

    for k in range(half // 256):
        XT[k * 256 : (k + 1) * 256, :] = X[1, :, k * 256 : (k + 1) * 256].T

    def couple(p):
        s, w = PAIRS[p]
        slot, cols = window(w)
        part = min(block, 256)
        for k in range(block // part):
            RAW[k * part : (k + 1) * part, :] = jnp.dot(
                XT[s * block + k * part : s * block + (k + 1) * part, :],
                X[slot, :, cols],
                preferred_element_type=f32,
            )

        def step(k, carry):
            at = pl.ds(pl.multiple_of(k * CHUNK, CHUNK), CHUNK)
            value = RAW[at, :] * TP[p, at, :]
            high = value.astype(bf16)
            CH[p, at, :] = high
            CL[p, at, :] = (value - high.astype(f32)).astype(bf16)
            return carry

        lax.fori_loop(0, block // CHUNK, step, 0, unroll=2)

    def split(values, w):
        high = values.astype(bf16)
        UH[w, 0:rows2, :] = high
        UH[w, rows2 : 2 * rows2, :] = (values - high.astype(f32)).astype(bf16)

    def product(p):
        s, w = PAIRS[p]
        full = lax.dot_general(UH[w], CH[p], NT, preferred_element_type=f32)
        low = lax.dot_general(UH[w, 0:rows2, :], CL[p], NT, preferred_element_type=f32)
        return (full[0:rows2] + full[rows2:] + low) * SC[p : p + 1, :]

    for copy in u_in:
        copy.wait_recv()
    for w in range(6):
        slot, cols = window(w)
        split(U[slot, :, cols], w)

    for s in range(2):
        cols = slice(s * block, (s + 1) * block)
        W[:, cols] = U[1, :, cols] * oerr[:, pl.ds(pl.multiple_of(c * half + s * block, block), block)]
    for p in range(10):
        if p == 4:
            for slot in (0, 2):
                for d in range(nmem):
                    forwarded(slot, d).wait_recv()
        couple(p)
        s = PAIRS[p][0]
        cols = slice(s * block, (s + 1) * block)
        W[:, cols] += product(p)
    V[1] = W[...]

    v_out = [
        remote(V.at[1], V.at[2], v_send.at[0], v_recv.at[0], left),
        remote(V.at[1], V.at[0], v_send.at[1], v_recv.at[1], right),
    ]
    for copy in v_out:
        copy.start()

    def lane_sums(value):
        total = value[:, 0:lanes]
        for k in range(1, half // lanes):
            total = total + value[:, k * lanes : (k + 1) * lanes]
        return total

    def total(count, one, two, one_sems, two_sems):
        row = jnp.sum(PP[0:count, :].T, axis=0, keepdims=True)
        out = []
        for buffer, index, size, peer, sems in (
            (one, i1, 2 * nx, peer1, one_sems),
            (two, z, nz, peer2, two_sems),
        ):
            buffer[pl.ds(index, 1), :] = row
            mine = buffer.at[pl.ds(index, 1), :]
            arrivals = []
            for d in range(1, size):
                copy = remote(mine, mine, sems[0].at[d], sems[1].at[d], peer(d))
                copy.start()
                out.append(copy)
                there = buffer.at[pl.ds(lax.rem(index + size - d, size), 1), :]
                arrivals.append(remote(mine, there, sems[0].at[d], sems[1].at[d], peer(d)))
            for copy in arrivals:
                copy.wait_recv()
            row = jnp.sum(buffer[...], axis=0, keepdims=True)
        return row, out

    def columns(lines):
        width = lines[0].shape[1]
        place = lax.broadcasted_iota(jnp.int32, (lanes, width), 0)
        table = jnp.broadcast_to(lines[0], (lanes, width))
        for k in range(1, len(lines)):
            table = jnp.where(place == k, lines[k], table)
        table = jnp.concatenate([table, jnp.zeros((lanes, lanes - width), f32)], axis=1)
        COEF[...] = table.T

    u0, u1 = U[1], V[1]
    PP[0:rows2, :] = lane_sums(u0 * u0)
    PP[rows2 : 2 * rows2, :] = lane_sums(u0 * u1)
    PP[2 * rows2 : 3 * rows2, :] = lane_sums(u1 * u1)
    PP[3 * rows2 : 4 * rows2, :] = jnp.zeros((rows2, lanes), f32)
    sums, s_out = total(4 * rows2, R1A, R2A, (r1_send, r1_recv), (r2_send, r2_recv))
    norm = sums[:, 0:rows2]
    size = norm / sums[:, rows2 : 2 * rows2]
    norm_next = size * size * sums[:, 2 * rows2 : 3 * rows2] - norm
    beta = norm_next / (norm + EPSILON)
    columns([size, beta])
    size_col = COEF[0:rows2, 0:1]
    beta_col = COEF[0:rows2, 1:2]

    v_in = [
        remote(V.at[1], V.at[2], v_send.at[0], v_recv.at[0], left),
        remote(V.at[1], V.at[0], v_send.at[1], v_recv.at[1], right),
    ]
    for copy in v_in:
        copy.wait_recv()
    for w in range(6):
        slot, cols = window(w)
        start = U[slot, :, cols]
        residual = start - size_col * V[slot, :, cols]
        direction = residual + beta_col * start
        split(direction, w)
        if slot == 1:
            W[:, cols] = direction
            W2[:, cols] = direction * oerr[:, pl.ds(pl.multiple_of(c * half + cols.start, block), block)]
    for p in range(10):
        s = PAIRS[p][0]
        cols = slice(s * block, (s + 1) * block)
        W2[:, cols] += product(p)

    w_copy = remote(W2.at[partner_rows, :], W3, w_send, w_recv, partner)
    w_copy.start()
    residual = U[1] - size_col * V[1]
    PP[0:rows2, :] = lane_sums(residual * residual)
    PP[rows2 : 2 * rows2, :] = lane_sums(W[...] * W2[...])
    sums, t_out = total(2 * rows2, R1B, R2B, (q1_send, q1_recv), (q2_send, q2_recv))
    size_next = sums[:, 0:rows2] / sums[:, rows2 : 2 * rows2]
    columns([size, beta, size_next])
    w_copy.wait_recv()
    size_here = COEF[core_rows, 0:1]
    beta_here = COEF[core_rows, 1:2]
    next_here = COEF[core_rows, 2:3]

    def finish(start, image, operated, where):
        residual = start - size_here * image
        direction = residual + beta_here * start
        x_out[:, where] = size_here * start + next_here * direction
        r_out[:, where] = residual - next_here * operated

    finish(innov[:, own_half], V[1, core_rows, :], W2[core_rows, :], own_half)
    finish(innov[:, other_half], V[2 - 2 * c, core_rows, :], W3[...], other_half)

    meta_back.wait_send()
    for copy in a_out + f_out + u_out + v_out + s_out + t_out + [w_copy]:
        copy.wait_send()


def body(anomalies, innovations, obs_error, positions, pair_far, block, nx):
    f32, bf16 = jnp.float32, jnp.bfloat16
    rows, width = anomalies.shape
    nobs, nmem = lax.axis_size("obs"), lax.axis_size("mem")
    nz = nobs // nx
    half, rows2, members, lanes = 2 * block, 2 * rows, rows * nmem, 128
    vmem = pl.BlockSpec(memory_space=pltpu.VMEM)
    dma = pltpu.SemaphoreType.DMA
    scratch = [
        pltpu.VMEM((3, members, half), bf16),
        pltpu.VMEM((half, members), bf16),
        pltpu.VMEM((3, rows2, half), f32),
        pltpu.VMEM((3, rows2, half), f32),
        pltpu.VMEM((6, 2 * rows2, block), bf16),
        pltpu.VMEM((10, block, block), bf16),
        pltpu.VMEM((10, block, block), bf16),
        pltpu.VMEM((10, block, block), f32),
        pltpu.VMEM((block, block), f32),
        pltpu.VMEM((2, half, lanes), f32),
        pltpu.VMEM((3, 8, half), f32),
        pltpu.VMEM((16, block), f32),
        pltpu.VMEM((4 * rows2, lanes), f32),
        pltpu.VMEM((rows2, half), f32),
        pltpu.VMEM((rows2, half), f32),
        pltpu.VMEM((rows, half), f32),
        pltpu.VMEM((lanes, lanes), f32),
        pltpu.VMEM((2 * nx, 4 * rows2), f32),
        pltpu.VMEM((nz, 4 * rows2), f32),
        pltpu.VMEM((2 * nx, 2 * rows2), f32),
        pltpu.VMEM((nz, 2 * rows2), f32),
        dma((nmem,)), dma((nmem,)),
        dma((2, nmem)), dma((2, nmem)),
        dma((4,)), dma((4,)),
        dma, dma,
        dma((2,)), dma((2,)),
        dma, dma,
        dma((2 * nx,)), dma((2 * nx,)), dma((nz,)), dma((nz,)),
        dma((2 * nx,)), dma((2 * nx,)), dma((nz,)), dma((nz,)),
    ]
    return pl.pallas_call(
        functools.partial(kernel, block, nobs, nmem, nx),
        out_shape=[jax.ShapeDtypeStruct((rows, width), f32)] * 2,
        in_specs=[vmem] * 4 + [pl.BlockSpec(memory_space=pltpu.SMEM)],
        out_specs=[vmem] * 2,
        scratch_shapes=scratch,
        compiler_params=pltpu.CompilerParams(
            collective_id=0, has_side_effects=True, vmem_limit_bytes=56 * 1024 * 1024
        ),
        name="filter_steps",
    )(anomalies, innovations, obs_error[None, :], positions, pair_far)


def solution(mesh, block=B, nx=NX):
    in_specs = (P("mem", "obs"), P("mem", "obs"), P("obs"), P(None, "obs"), P("obs"))
    out_specs = (P("mem", "obs"), P("mem", "obs"))
    return jax.shard_map(
        functools.partial(body, block=block, nx=nx),
        mesh=mesh,
        in_specs=in_specs,
        out_specs=out_specs,
        check_vma=False,
    )
```

```python
import functools
import math

import jax
import jax.numpy as jnp
from jax import lax
from jax.experimental import pallas as pl
from jax.experimental.pallas import tpu as pltpu
from jax.sharding import PartitionSpec as P

B = 512
NX = 4
EPSILON = 1e-06
ROOT2 = math.sqrt(2.0)
SCALE = 48.0 * ROOT2
MESH = pl.DeviceIdType.MESH
LANES = 128
CHUNK = 32


def remote(src, dst, send, recv, device):
    return pltpu.make_async_remote_copy(
        src_ref=src, dst_ref=dst, send_sem=send, recv_sem=recv, device_id=device, device_id_type=MESH
    )


def kernel(
    block, nobs, nmem, nx,
    anom, innov, oerr, places, far, u1_out, u2_out, c_out,
    X, XT, U, V, UH, CH, CL, TP, PI, META, PP, W2, W3, SB, SR, G,
    a_send, a_recv, f_send, f_recv, u_send, u_recv, m_send, m_recv, v_send, v_recv, w_send, w_recv,
    e_send, e_recv, g_send, g_recv, reach, o_sem,
):
    f32, bf16 = jnp.float32, jnp.bfloat16
    half = 2 * block
    rows = anom.shape[0]
    rows2 = 2 * rows
    nz = nobs // nx
    o = lax.axis_index("obs")
    mm = lax.axis_index("mem")
    c = lax.rem(mm, 2)
    y2 = mm - c
    up = lax.rem(y2 + 2, nmem)
    down = lax.rem(y2 + nmem - 2, nmem)
    across_y = lax.rem(y2 + nmem // 2, nmem)
    pm = y2 + 1 - c
    z = lax.div(o, nx)
    x = lax.rem(o, nx)
    left = (lax.rem(o + nobs - 1 + c, nobs), pm)
    right = (lax.rem(o + c, nobs), pm)
    partner = (o, pm)
    far_to = (lax.rem(o + nobs + 1 - 2 * c, nobs), mm)
    far_from = (lax.rem(o + nobs - 1 + 2 * c, nobs), mm)
    off_chip = (lax.rem(o + nobs - 1 + 2 * c, nobs), pm)

    def peer(dz, dx):
        return (lax.rem(z + dz + nz, nz) * nx + lax.rem(x + dx + nx, nx), mm)

    barrier = pltpu.get_barrier_semaphore()
    near = [partner, left, right, far_to, far_from]
    near += [(o, y + k) for y in (up, down) for k in range(2)]
    near += [peer(0, dx) for dx in range(1, nx)]
    near += [peer(dz, 0) for dz in sorted({1, nz - 1})]
    for device in near:
        pl.semaphore_signal(barrier, inc=1, device_id=device, device_id_type=MESH)

    own_rows = pl.ds(pl.multiple_of(mm * rows, rows), rows)
    core_rows = pl.ds(pl.multiple_of(c * rows, rows), rows)
    partner_rows = pl.ds(pl.multiple_of((1 - c) * rows, rows), rows)
    own_half = pl.ds(pl.multiple_of(c * half, half), half)
    other_half = pl.ds(pl.multiple_of((1 - c) * half, half), half)
    pf = places[...].astype(f32) * ROOT2
    for h in range(2):
        flags = jnp.concatenate(
            [jnp.full((1, block), far[2 * h + b].astype(f32), f32) for b in range(2)], axis=1
        )
        META[1 - c + h] = jnp.concatenate(
            [pf[:, h * half : (h + 1) * half], flags, jnp.zeros((5, half), f32)], axis=0
        )
    X[1, own_rows, :] = anom[:, own_half]
    pl.semaphore_wait(barrier, len(near))

    steps = [step for step in (1, 2, 4, 8) if 2 * step <= nz]

    def tell(k):
        for dz in sorted({steps[k], nz - steps[k]}):
            pl.semaphore_signal(reach.at[k], inc=1, device_id=peer(dz, 0), device_id_type=MESH)

    def hear(k):
        pl.semaphore_wait(reach.at[k], len({steps[k], nz - steps[k]}))

    def widen(k):
        if k < len(steps):
            hear(k)
            if k + 1 < len(steps):
                tell(k + 1)

    meta_copy = remote(META.at[1], META.at[2 - 2 * c], m_send, m_recv, off_chip)
    meta_copy.start()
    meta_back = remote(META.at[1], META.at[2 * c], m_send, m_recv, off_chip)

    def half_of(core):
        return pl.ds(pl.multiple_of(core * half, half), half)

    def rows_of(member):
        return pl.ds(pl.multiple_of(member * rows, rows), rows)

    a_out = []
    for core in range(2):
        k = lax.rem(c + core, 2)
        a_out.append(
            remote(anom.at[:, half_of(k)], X.at[1, own_rows, :], a_send.at[1 + core], a_recv.at[1 + c], (o, up + k))
        )
        a_out.append(
            remote(anom.at[:, half_of(k)], X.at[1, own_rows, :], a_send.at[3 + core], a_recv.at[3 + c], (o, down + k))
        )
    a_out.append(remote(anom.at[:, other_half], X.at[1, own_rows, :], a_send.at[0], a_recv.at[0], partner))
    for copy in a_out:
        copy.start()

    u_out = [
        remote(innov.at[:, own_half], U.at[2, core_rows, :], u_send.at[0], u_recv.at[0], left),
        remote(innov.at[:, own_half], U.at[0, core_rows, :], u_send.at[1], u_recv.at[1], right),
        remote(innov.at[:, other_half], U.at[1, core_rows, :], u_send.at[2], u_recv.at[2], partner),
        remote(innov.at[:, other_half], U.at[2 * c, core_rows, :], u_send.at[3], u_recv.at[3], far_to),
    ]
    u_in = [
        remote(innov.at[:, own_half], U.at[2, partner_rows, :], u_send.at[0], u_recv.at[0], left),
        remote(innov.at[:, own_half], U.at[0, partner_rows, :], u_send.at[1], u_recv.at[1], right),
        remote(innov.at[:, other_half], U.at[1, partner_rows, :], u_send.at[2], u_recv.at[2], partner),
        remote(innov.at[:, other_half], U.at[2 * c, core_rows, :], u_send.at[3], u_recv.at[3], far_to),
    ]

    sources = [mm, pm, down, down + 1, up, up + 1, across_y, across_y + 1]
    f_out, relays = [], []

    def arrived(k):
        piece = rows_of(sources[k])
        remote(anom.at[:, own_half], X.at[1, piece, :], a_send.at[k - 1], a_recv.at[k - 1], partner).wait_recv()

    def forward(k):
        piece = rows_of(sources[k])
        if k > 0:
            arrived(k)
        if k == 2:
            relays.append(remote(X.at[1, piece, :], X.at[1, piece, :], a_send.at[5], a_recv.at[5], (o, up + c)))
            relays[-1].start()
        if k == 5:
            relays.append(remote(X.at[1, piece, :], X.at[1, piece, :], a_send.at[6], a_recv.at[6], (o, down + c)))
            relays[-1].start()
        one = remote(X.at[1, piece, :], X.at[2, piece, :], f_send.at[0, k], f_recv.at[0], left)
        two = remote(X.at[1, piece, :], X.at[0, piece, :], f_send.at[1, k], f_recv.at[1], right)
        one.start()
        two.start()
        f_out.extend([one, two])

    forward(0)
    for copy in u_out:
        copy.start()
    tell(0)
    for h in range(2):
        U[1 - c + h, core_rows, :] = innov[:, h * half : (h + 1) * half]

    def columns(slot):
        for k in range(half // LANES):
            for axis in range(2):
                line = META[slot, axis : axis + 1, k * LANES : (k + 1) * LANES]
                at = slot * half + k * LANES
                PI[axis, at : at + LANES, :] = jnp.broadcast_to(line, (LANES, LANES)).T

    def taper(s, w):
        offset = w - 2 - s
        cols = slice(s * block, (s + 1) * block)
        along = META[1, 0:1, cols] - offset * ROOT2
        across = META[1, 1:2, cols]
        close = abs(offset) < 2
        base = (w - s) * block
        times = block // LANES

        def step(k, carry):
            at = pl.multiple_of(k * CHUNK, CHUNK)
            theirs = pl.ds(w * block + at, CHUNK)
            g = jnp.concatenate([PI[0, theirs, :]] * times, axis=1) - along
            h = jnp.concatenate([PI[1, theirs, :]] * times, axis=1) - across
            square = g * g + h * h
            if close:
                square = jnp.maximum(square, 1e-30)
            inverse = lax.rsqrt(square)
            y = square * inverse
            rest = jnp.maximum(2.0 * ROOT2 - y, 0.0)
            rest = rest * rest
            value = (rest * rest) * ((y - inverse) + 2.0 * ROOT2)
            if close:
                inner = (-3.0 * y + 0.125 * SCALE) * y + 0.3125 * SCALE / ROOT2
                inner = (inner * y - (5.0 / 6.0) * SCALE) * square + SCALE
                value = jnp.maximum(value, inner)
            TP[s, pl.ds(base + at, CHUNK), :] = value
            return carry

        lax.fori_loop(0, block // CHUNK, step, 0, unroll=2)

    columns(1)
    taper(0, 2)
    forward(1)
    taper(0, 3)
    taper(1, 2)
    forward(2)
    taper(1, 3)
    forward(5)
    meta_back.wait_recv()
    columns(0)
    columns(2)
    taper(0, 1)
    forward(3)
    taper(1, 4)
    forward(4)
    widen(0)
    taper(0, 0)
    taper(0, 4)
    taper(1, 1)
    taper(1, 5)
    widen(1)

    first = jnp.where(2 * o + c > 0, 1.0, 0.0).astype(f32)
    last = jnp.where(2 * o + c < 2 * nobs - 1, 1.0, 0.0).astype(f32)

    def turn(slot):
        part = 2 * LANES
        for k in range(half // part):
            at = slot * half + k * part
            XT[at : at + part, :] = X[slot, :, k * part : (k + 1) * part].T

    def couple(s, w):
        offset = w - 2 - s
        cols = slice(s * block, (s + 1) * block)
        at = slice((w - s) * block, (w - s + 1) * block)
        value = jnp.dot(
            XT[w * block : (w + 1) * block, :], X[1, :, cols], preferred_element_type=f32
        ) * TP[s, at, :]
        if w < 2 or w > 3:
            line = jnp.full((1, block), 1.0, f32) * (first if w < 2 else last)
            if offset == 2:
                line = line * META[1, 2:3, cols]
            if offset == -2:
                line = line * META[0, 2:3, cols]
            value = value * line
        high = value.astype(bf16)
        CH[s, at, :] = high
        CL[s, at, :] = (value - high.astype(f32)).astype(bf16)

    def split(values, slot):
        cols = slice(slot * half, (slot + 1) * half)
        high = values.astype(bf16)
        UH[0:rows2, cols] = high
        UH[rows2 : 2 * rows2, cols] = (values - high.astype(f32)).astype(bf16)

    factor = 1.0 / (SCALE * (rows * nmem - 1))

    def product(s, begin, end):
        cols = slice(begin * block, end * block)
        at = slice((begin - s) * block, (end - s) * block)
        full = jnp.dot(UH[:, cols], CH[s, at, :], preferred_element_type=f32)
        low = jnp.dot(UH[0:rows2, cols], CL[s, at, :], preferred_element_type=f32)
        return (full[0:rows2] + full[rows2:] + low) * factor

    def noise(s):
        return oerr[:, pl.ds(pl.multiple_of(c * half + s * block, block), block)]

    for k in (6, 7):
        forward(k)
    turn(1)
    for s in range(2):
        for w in (2, 3):
            couple(s, w)
    widen(2)
    u_in[2].wait_recv()
    split(U[1], 1)
    for s in range(2):
        cols = slice(s * block, (s + 1) * block)
        V[1, :, cols] = U[1, :, cols] * noise(s) + product(s, 2, 4)
    for k in (0, 1, 3):
        u_in[k].wait_recv()
    split(U[0], 0)
    split(U[2], 2)
    for slot, way in ((0, 1), (2, 0)):
        remote(X.at[1], X.at[slot], f_send.at[0, 0], f_recv.at[way], partner).wait_recv()
        turn(slot)
    for s in range(2):
        for w in range(s, 2):
            couple(s, w)
        for w in range(4, s + 5):
            couple(s, w)

    v_out = []
    for s in range(2):
        cols = slice(s * block, (s + 1) * block)
        V[1, :, cols] += product(s, s, 2) + product(s, 4, s + 5)
        v_out.append(remote(V.at[1, :, cols], V.at[2, :, cols], v_send.at[0, s], v_recv.at[0, s], left))
        v_out.append(remote(V.at[1, :, cols], V.at[0, :, cols], v_send.at[1, s], v_recv.at[1, s], right))
        v_out[-2].start()
        v_out[-1].start()

    widen(3)
    u1_copy = [pltpu.make_async_copy(V.at[1, core_rows, :], u1_out.at[:, own_half], o_sem.at[0])]
    u1_copy[0].start()

    def lane_sums(d, value):
        total = value[:, 0:LANES]
        for k in range(1, half // LANES):
            total = total + value[:, k * LANES : (k + 1) * LANES]
        for h in range(2):
            PP[(4 * h + d) * rows : (4 * h + d + 1) * rows, :] = total[h * rows : (h + 1) * rows]

    split(V[1], 1)
    for s in range(2):
        cols = slice(s * block, (s + 1) * block)
        W2[:, cols] = V[1, :, cols] * noise(s) + product(s, 2, 4)
    lane_sums(0, U[1] * U[1])
    lane_sums(1, U[1] * V[1])
    lane_sums(2, V[1] * V[1])
    for way, slot in ((1, 0), (0, 2)):
        for s in range(2):
            cols = slice(s * block, (s + 1) * block)
            remote(V.at[1, :, cols], V.at[slot, :, cols], v_send.at[way, s], v_recv.at[way, s], partner).wait_recv()
        split(V[slot], slot)
    for s in range(2):
        cols = slice(s * block, (s + 1) * block)
        W2[:, cols] += product(s, s, 2) + product(s, 4, s + 5)

    lane_sums(3, V[1] * W2[...])
    row = jnp.sum(PP[...].T, axis=0, keepdims=True)
    SB[0:1, :] = row[:, 0 : 4 * rows]
    SB[1:2, :] = row[:, 4 * rows :]
    e_copy = remote(SB.at[pl.ds(1 - c, 1), :], SR, e_send, e_recv, partner)
    e_copy.start()
    w_copy = remote(W2.at[partner_rows, :], W3, w_send, w_recv, partner)
    w_copy.start()
    e_copy.wait_recv()
    G[pl.ds(o, 1), :] = SB[pl.ds(c, 1), :] + SR[...]
    mine = G.at[pl.ds(o, 1), :]
    offsets = [(dz, dx) for dz in range(nz) for dx in range(nx) if dz or dx]
    offsets.sort(key=lambda d: -(min(d[0], nz - d[0]) + min(d[1], nx - d[1])))
    for dz, dx in offsets:
        remote(mine, mine, g_send, g_recv, peer(dz, dx)).start()
    u1_copy.append(
        pltpu.make_async_copy(V.at[2 - 2 * c, core_rows, :], u1_out.at[:, other_half], o_sem.at[1])
    )
    u2_copy = [
        pltpu.make_async_copy(W2.at[core_rows, :], u2_out.at[:, own_half], o_sem.at[2]),
        pltpu.make_async_copy(W3, u2_out.at[:, other_half], o_sem.at[3]),
    ]
    u1_copy[1].start()
    u2_copy[0].start()
    w_copy.wait_recv()
    u2_copy[1].start()
    rest = G.at[0 : nobs - 1, :]
    remote(rest, rest, g_send, g_recv, partner).wait_recv()
    sums = jnp.sum(G[...], axis=0, keepdims=True)

    norm = sums[:, 0:rows]
    cross = sums[:, rows : 2 * rows]
    image = sums[:, 2 * rows : 3 * rows]
    size = norm / cross
    norm_next = size * size * image - norm
    more = 1.0 + norm_next / (norm + EPSILON)
    curve = (more * cross - 2.0 * size * image) * more + size * size * sums[:, 3 * rows :]
    size_next = norm_next / curve
    place = lax.broadcasted_iota(jnp.int32, (LANES, rows), 0)
    table = jnp.where(place == 0, size + size_next * more, size * size_next)
    table = jnp.concatenate([table, jnp.zeros((LANES, LANES - rows), f32)], axis=1)
    c_out[...] = table.T[0:rows, :]

    for copy in [meta_copy] + a_out + relays + f_out + u_out + v_out + [e_copy, w_copy]:
        copy.wait_send()
    remote(rest, rest, g_send, g_recv, partner).wait_send()
    for copy in u1_copy + u2_copy:
        copy.wait()


def body(anomalies, innovations, obs_error, positions, pair_far, block, nx):
    f32, bf16 = jnp.float32, jnp.bfloat16
    rows, width = anomalies.shape
    nobs, nmem = lax.axis_size("obs"), lax.axis_size("mem")
    half, rows2, members = 2 * block, 2 * rows, rows * nmem
    vmem = pl.BlockSpec(memory_space=pltpu.VMEM)
    whole = pl.BlockSpec(memory_space=pl.ANY)
    dma = pltpu.SemaphoreType.DMA
    scratch = [
        pltpu.VMEM((3, members, half), bf16),
        pltpu.VMEM((3 * half, members), bf16),
        pltpu.VMEM((3, rows2, half), f32),
        pltpu.VMEM((3, rows2, half), f32),
        pltpu.VMEM((2 * rows2, 3 * half), bf16),
        pltpu.VMEM((2, 5 * block, block), bf16),
        pltpu.VMEM((2, 5 * block, block), bf16),
        pltpu.VMEM((2, 5 * block, block), f32),
        pltpu.VMEM((2, 3 * half, LANES), f32),
        pltpu.VMEM((3, 8, half), f32),
        pltpu.VMEM((8 * rows, LANES), f32),
        pltpu.VMEM((rows2, half), f32),
        pltpu.VMEM((rows, half), f32),
        pltpu.VMEM((2, 4 * rows), f32),
        pltpu.VMEM((1, 4 * rows), f32),
        pltpu.VMEM((nobs, 4 * rows), f32),
        dma((7,)), dma((7,)),
        dma((2, 8)), dma((2,)),
        dma((4,)), dma((4,)),
        dma, dma,
        dma((2, 2)), dma((2, 2)),
        dma, dma,
        dma, dma,
        dma, dma,
        pltpu.SemaphoreType.REGULAR((4,)),
        dma((4,)),
    ]
    image, again, factors = pl.pallas_call(
        functools.partial(kernel, block, nobs, nmem, nx),
        out_shape=[jax.ShapeDtypeStruct((rows, width), f32)] * 2 + [jax.ShapeDtypeStruct((rows, LANES), f32)],
        in_specs=[vmem] * 4 + [pl.BlockSpec(memory_space=pltpu.SMEM)],
        out_specs=[whole, whole, vmem],
        scratch_shapes=scratch,
        compiler_params=pltpu.CompilerParams(
            collective_id=0, has_side_effects=True, vmem_limit_bytes=56 * 1024 * 1024
        ),
        name="filter_steps",
    )(anomalies, innovations, obs_error[None, :], positions, pair_far)
    linear, square = factors[:, 0:1], factors[:, 1:2]
    return (
        linear * innovations - square * image,
        innovations - linear * image + square * again,
    )


def solution(mesh, block=B, nx=NX):
    in_specs = (P("mem", "obs"), P("mem", "obs"), P("obs"), P(None, "obs"), P("obs"))
    out_specs = (P("mem", "obs"), P("mem", "obs"))
    return jax.shard_map(
        functools.partial(body, block=block, nx=nx),
        mesh=mesh,
        in_specs=in_specs,
        out_specs=out_specs,
        check_vma=False,
    )
```

```python
import functools
import math

import jax
import jax.numpy as jnp
from jax import lax
from jax.experimental import pallas as pl
from jax.experimental.pallas import tpu as pltpu
from jax.sharding import PartitionSpec as P

B = 512
NX = 4
EPSILON = 1e-06
ROOT2 = math.sqrt(2.0)
SCALE = 48.0 * ROOT2
MESH = pl.DeviceIdType.MESH
LANES = 128
CHUNK = 32


def remote(src, dst, send, recv, device):
    return pltpu.make_async_remote_copy(
        src_ref=src, dst_ref=dst, send_sem=send, recv_sem=recv, device_id=device, device_id_type=MESH
    )


def kernel(
    block, nobs, nmem, nx,
    anom, innov, oerr, places, far, u1_out, u2_out, c_out,
    X, XT, U, V, UH, CH, CL, TP, PI, META, PP, W2, W3, SB, SR, G,
    a_send, a_recv, f_send, f_recv, u_send, u_recv, m_send, m_recv, v_send, v_recv, w_send, w_recv,
    e_send, e_recv, g_send, g_recv, reach, o_sem,
):
    f32, bf16 = jnp.float32, jnp.bfloat16
    half = 2 * block
    rows = anom.shape[0]
    rows2 = 2 * rows
    nz = nobs // nx
    o = lax.axis_index("obs")
    mm = lax.axis_index("mem")
    c = lax.rem(mm, 2)
    y2 = mm - c
    up = lax.rem(y2 + 2, nmem)
    down = lax.rem(y2 + nmem - 2, nmem)
    across_y = lax.rem(y2 + nmem // 2, nmem)
    pm = y2 + 1 - c
    z = lax.div(o, nx)
    x = lax.rem(o, nx)
    left = (lax.rem(o + nobs - 1 + c, nobs), pm)
    right = (lax.rem(o + c, nobs), pm)
    partner = (o, pm)
    far_to = (lax.rem(o + nobs + 1 - 2 * c, nobs), mm)
    far_from = (lax.rem(o + nobs - 1 + 2 * c, nobs), mm)
    off_chip = (lax.rem(o + nobs - 1 + 2 * c, nobs), pm)

    def peer(dz, dx):
        return (lax.rem(z + dz + nz, nz) * nx + lax.rem(x + dx + nx, nx), mm)

    barrier = pltpu.get_barrier_semaphore()
    near = [partner, left, right, far_to, far_from]
    near += [(o, y + k) for y in (up, down) for k in range(2)]
    near += [peer(0, dx) for dx in range(1, nx)]
    near += [peer(dz, 0) for dz in sorted({1, nz - 1})]
    for device in near:
        pl.semaphore_signal(barrier, inc=1, device_id=device, device_id_type=MESH)

    own_rows = pl.ds(pl.multiple_of(mm * rows, rows), rows)
    core_rows = pl.ds(pl.multiple_of(c * rows, rows), rows)
    partner_rows = pl.ds(pl.multiple_of((1 - c) * rows, rows), rows)
    own_half = pl.ds(pl.multiple_of(c * half, half), half)
    other_half = pl.ds(pl.multiple_of((1 - c) * half, half), half)
    pf = places[...].astype(f32) * ROOT2
    for h in range(2):
        flags = jnp.concatenate(
            [jnp.full((1, block), far[2 * h + b].astype(f32), f32) for b in range(2)], axis=1
        )
        META[1 - c + h] = jnp.concatenate(
            [pf[:, h * half : (h + 1) * half], flags, jnp.zeros((5, half), f32)], axis=0
        )
    X[1, own_rows, :] = anom[:, own_half]
    pl.semaphore_wait(barrier, len(near))

    steps = [step for step in (1, 2, 4, 8) if 2 * step <= nz]

    def tell(k):
        for dz in sorted({steps[k], nz - steps[k]}):
            pl.semaphore_signal(reach.at[k], inc=1, device_id=peer(dz, 0), device_id_type=MESH)

    def hear(k):
        pl.semaphore_wait(reach.at[k], len({steps[k], nz - steps[k]}))

    def widen(k):
        if k < len(steps):
            hear(k)
            if k + 1 < len(steps):
                tell(k + 1)

    meta_copy = remote(META.at[1], META.at[2 - 2 * c], m_send, m_recv, off_chip)
    meta_copy.start()
    meta_back = remote(META.at[1], META.at[2 * c], m_send, m_recv, off_chip)

    def half_of(core):
        return pl.ds(pl.multiple_of(core * half, half), half)

    def rows_of(member):
        return pl.ds(pl.multiple_of(member * rows, rows), rows)

    a_out = []
    for way, slot in ((up + c * (down - up), 1 + 3 * c), (down + c * (up - down), 3 - c)):
        for core in range(2):
            k = lax.rem(c + core, 2)
            copy = remote(
                anom.at[:, half_of(k)], X.at[1, own_rows, :], a_send.at[len(a_out) + 1], a_recv.at[slot], (o, way + k)
            )
            a_out.append(copy)
    a_out.append(remote(anom.at[:, other_half], X.at[1, own_rows, :], a_send.at[0], a_recv.at[0], partner))
    for copy in a_out:
        copy.start()

    u_out = [
        remote(innov.at[:, own_half], U.at[2, core_rows, :], u_send.at[0], u_recv.at[0], left),
        remote(innov.at[:, own_half], U.at[0, core_rows, :], u_send.at[1], u_recv.at[1], right),
        remote(innov.at[:, other_half], U.at[1, core_rows, :], u_send.at[2], u_recv.at[2], partner),
        remote(innov.at[:, other_half], U.at[2 * c, core_rows, :], u_send.at[3], u_recv.at[3], far_to),
    ]
    u_in = [
        remote(innov.at[:, own_half], U.at[2, partner_rows, :], u_send.at[0], u_recv.at[0], left),
        remote(innov.at[:, own_half], U.at[0, partner_rows, :], u_send.at[1], u_recv.at[1], right),
        remote(innov.at[:, other_half], U.at[1, partner_rows, :], u_send.at[2], u_recv.at[2], partner),
        remote(innov.at[:, other_half], U.at[2 * c, core_rows, :], u_send.at[3], u_recv.at[3], far_to),
    ]

    sources = [mm, pm, down, down + 1, up, up + 1, across_y, across_y + 1]
    f_out, relays = [], []

    def arrived(k):
        piece = rows_of(sources[k])
        remote(anom.at[:, own_half], X.at[1, piece, :], a_send.at[k - 1], a_recv.at[k - 1], partner).wait_recv()

    def forward(k):
        piece = rows_of(sources[k])
        if k > 0:
            arrived(k)
        if k == 2:
            relays.append(remote(X.at[1, piece, :], X.at[1, piece, :], a_send.at[5], a_recv.at[5], (o, up + c)))
            relays[-1].start()
        if k == 5:
            relays.append(remote(X.at[1, piece, :], X.at[1, piece, :], a_send.at[6], a_recv.at[6], (o, down + c)))
            relays[-1].start()
        one = remote(X.at[1, piece, :], X.at[2, piece, :], f_send.at[0, k], f_recv.at[0], left)
        two = remote(X.at[1, piece, :], X.at[0, piece, :], f_send.at[1, k], f_recv.at[1], right)
        one.start()
        two.start()
        f_out.extend([one, two])

    forward(0)
    for copy in u_out:
        copy.start()
    tell(0)
    for h in range(2):
        U[1 - c + h, core_rows, :] = innov[:, h * half : (h + 1) * half]

    off_side, on_side = c, 1 - c

    def span(start, size):
        return pl.ds(start if isinstance(start, int) else pl.multiple_of(start, size), size)

    def columns(slot):
        for k in range(half // LANES):
            for axis in range(2):
                line = META[slot, axis : axis + 1, k * LANES : (k + 1) * LANES]
                PI[axis, span(slot * half + k * LANES, LANES), :] = jnp.broadcast_to(line, (LANES, LANES)).T

    def taper(s, w, close):
        cols = span(s * block, block)
        shift = (w - 2 - s) * ROOT2 if isinstance(w, int) else (w - 2 - s).astype(f32) * ROOT2
        along = META[1, 0:1, cols] - shift
        across = META[1, 1:2, cols]
        times = block // LANES

        def step(k, carry):
            theirs = span(w * block + k * CHUNK, CHUNK)
            g = jnp.concatenate([PI[0, theirs, :]] * times, axis=1) - along
            h = jnp.concatenate([PI[1, theirs, :]] * times, axis=1) - across
            square = g * g + h * h
            if close:
                square = jnp.maximum(square, 1e-30)
            inverse = lax.rsqrt(square)
            y = square * inverse
            rest = jnp.maximum(2.0 * ROOT2 - y, 0.0)
            rest = rest * rest
            value = (rest * rest) * ((y - inverse) + 2.0 * ROOT2)
            if close:
                inner = (-3.0 * y + 0.125 * SCALE) * y + 0.3125 * SCALE / ROOT2
                inner = (inner * y - (5.0 / 6.0) * SCALE) * square + SCALE
                value = jnp.maximum(value, inner)
            TP[s, span((w - s) * block + k * CHUNK, CHUNK), :] = value
            return carry

        lax.fori_loop(0, block // CHUNK, step, 0, unroll=2)

    def cross_pair(side):
        return 1 - side, 1 + 3 * side

    def next_pair(side):
        return side, 1 + 3 * side

    def outer_pair(side):
        return side, 5 * side

    columns(1)
    taper(0, 2, True)
    columns(2 * on_side)
    taper(0, 3, True)
    forward(1)
    taper(1, 3, True)
    taper(*next_pair(on_side), True)
    forward(2)
    taper(*cross_pair(on_side), False)
    forward(5)
    taper(*outer_pair(on_side), False)
    forward(3)
    forward(4)
    widen(0)
    meta_back.wait_recv()
    columns(2 * off_side)
    taper(*cross_pair(off_side), False)
    taper(*next_pair(off_side), True)
    forward(6)
    taper(*outer_pair(off_side), False)
    forward(7)
    widen(1)

    def turn(slot):
        part = 2 * LANES
        for k in range(half // part):
            XT[span(slot * half + k * part, part), :] = X[slot, :, k * part : (k + 1) * part].T

    def couple(s, w, factor=None):
        at = span((w - s) * block, block)
        value = jnp.dot(
            XT[span(w * block, block), :], X[1, :, span(s * block, block)], preferred_element_type=f32
        ) * TP[s, at, :]
        if factor is not None:
            value = value * factor
        high = value.astype(bf16)
        CH[s, at, :] = high
        CL[s, at, :] = (value - high.astype(f32)).astype(bf16)

    def present(side):
        chain = 2 * o + c
        edge = jnp.where(side == 0, 0, 2 * nobs - 1)
        return jnp.where(chain == edge, 0.0, 1.0).astype(f32)

    def listed(s, side):
        return META[side, 2:3, span(s * block, block)] * present(side)

    def split(values, slot):
        cols = span(slot * half, half)
        high = values.astype(bf16)
        UH[0:rows2, cols] = high
        UH[rows2 : 2 * rows2, cols] = (values - high.astype(f32)).astype(bf16)

    factor = 1.0 / (SCALE * (rows * nmem - 1))

    def multiply(s, first_row, first_block, count):
        cols = span(first_block * block, count * block) if isinstance(first_block, int) else pl.ds(
            pl.multiple_of(first_block * block, block), count * block
        )
        at = pl.ds(pl.multiple_of(first_row * block, block), count * block)
        full = jnp.dot(UH[:, cols], CH[s, at, :], preferred_element_type=f32)
        low = jnp.dot(UH[0:rows2, cols], CL[s, at, :], preferred_element_type=f32)
        return (full[0:rows2] + full[rows2:] + low) * factor

    def own_product(s):
        if s == 0:
            return multiply(0, 2, 2, 2)
        cols = slice(2 * block, 3 * block)
        at = slice(3 * block, 4 * block)
        turned = (((1,), (1,)), ((), ()))
        full = lax.dot_general(UH[:, cols], CH[0, at, :], turned, preferred_element_type=f32)
        low = lax.dot_general(UH[0:rows2, cols], CL[0, at, :], turned, preferred_element_type=f32)
        return multiply(1, 2, 3, 1) + (full[0:rows2] + full[rows2:] + low) * factor

    def cross_product(side):
        return multiply(1 - side, 4 * side, 1 + 3 * side, 1)

    def side_product(side):
        return multiply(side, 3 * side, 4 * side, 2)

    def noise(s):
        return oerr[:, pl.ds(pl.multiple_of(c * half + s * block, block), block)]

    def wait_anomalies(side):
        remote(X.at[1], X.at[2 * side], f_send.at[0, 0], f_recv.at[1 - side], partner).wait_recv()

    def couple_cross(side):
        s, w = cross_pair(side)
        couple(s, w, listed(s, side))

    def couple_side(side):
        couple(*next_pair(side), present(side))
        s, w = outer_pair(side)
        couple(s, w, listed(s, side))

    turn(1)
    for s, w in ((0, 2), (0, 3), (1, 3)):
        couple(s, w)
    u_in[2].wait_recv()
    split(U[1], 1)
    for s in range(2):
        cols = slice(s * block, (s + 1) * block)
        V[1, :, cols] = U[1, :, cols] * noise(s) + own_product(s)
    remote(innov.at[:, own_half], U.at[2 * on_side, partner_rows, :], u_send.at[0], u_recv.at[1 - on_side], partner).wait_recv()
    split(U[2 * on_side], 2 * on_side)
    wait_anomalies(on_side)
    turn(2 * on_side)
    couple_cross(on_side)
    couple_side(on_side)
    V[1, :, span((1 - on_side) * block, block)] += cross_product(on_side)
    V[1, :, span(on_side * block, block)] += side_product(on_side)
    widen(2)
    remote(innov.at[:, own_half], U.at[2 * off_side, partner_rows, :], u_send.at[0], u_recv.at[1 - off_side], partner).wait_recv()
    u_in[3].wait_recv()
    split(U[2 * off_side], 2 * off_side)
    wait_anomalies(off_side)
    turn(2 * off_side)

    v_out = []

    def send_image(s, part):
        cols = span(s * block, block)
        v_out.append(remote(V.at[1, :, cols], V.at[2, :, cols], v_send.at[0, part], v_recv.at[0, part], left))
        v_out.append(remote(V.at[1, :, cols], V.at[0, :, cols], v_send.at[1, part], v_recv.at[1, part], right))
        v_out[-2].start()
        v_out[-1].start()

    couple_cross(off_side)
    V[1, :, span((1 - off_side) * block, block)] += cross_product(off_side)
    send_image(1 - off_side, 0)
    couple_side(off_side)
    V[1, :, span(off_side * block, block)] += side_product(off_side)
    send_image(off_side, 1)

    u1_copy = [pltpu.make_async_copy(V.at[1, core_rows, :], u1_out.at[:, own_half], o_sem.at[0])]
    u1_copy[0].start()

    def lane_sums(d, value):
        total = value[:, 0:LANES]
        for k in range(1, half // LANES):
            total = total + value[:, k * LANES : (k + 1) * LANES]
        for h in range(2):
            PP[(4 * h + d) * rows : (4 * h + d + 1) * rows, :] = total[h * rows : (h + 1) * rows]

    def wait_image(side):
        for part in range(2):
            s = c if part == 0 else 1 - c
            cols = span(s * block, block)
            remote(
                V.at[1, :, cols], V.at[2 * side, :, cols], v_send.at[0, part], v_recv.at[1 - side, part], partner
            ).wait_recv()
        split(V[2 * side], 2 * side)

    split(V[1], 1)
    for s in range(2):
        cols = slice(s * block, (s + 1) * block)
        W2[:, cols] = V[1, :, cols] * noise(s) + own_product(s)
    lane_sums(0, U[1] * U[1])
    lane_sums(1, U[1] * V[1])
    lane_sums(2, V[1] * V[1])
    wait_image(on_side)
    W2[:, span((1 - on_side) * block, block)] += cross_product(on_side)
    W2[:, span(on_side * block, block)] += side_product(on_side)
    widen(3)
    wait_image(off_side)
    W2[:, span((1 - off_side) * block, block)] += cross_product(off_side)
    W2[:, span(off_side * block, block)] += side_product(off_side)

    lane_sums(3, V[1] * W2[...])
    row = jnp.sum(PP[...].T, axis=0, keepdims=True)
    SB[0:1, :] = row[:, 0 : 4 * rows]
    SB[1:2, :] = row[:, 4 * rows :]
    e_copy = remote(SB.at[pl.ds(1 - c, 1), :], SR, e_send, e_recv, partner)
    e_copy.start()
    w_copy = remote(W2.at[partner_rows, :], W3, w_send, w_recv, partner)
    w_copy.start()
    e_copy.wait_recv()
    G[pl.ds(o, 1), :] = SB[pl.ds(c, 1), :] + SR[...]
    mine = G.at[pl.ds(o, 1), :]
    offsets = [(dz, dx) for dz in range(nz) for dx in range(nx) if dz or dx]
    offsets.sort(key=lambda d: -(min(d[0], nz - d[0]) + min(d[1], nx - d[1])))
    for dz, dx in offsets:
        remote(mine, mine, g_send, g_recv, peer(dz, dx)).start()
    u1_copy.append(
        pltpu.make_async_copy(V.at[2 - 2 * c, core_rows, :], u1_out.at[:, other_half], o_sem.at[1])
    )
    u2_copy = [
        pltpu.make_async_copy(W2.at[core_rows, :], u2_out.at[:, own_half], o_sem.at[2]),
        pltpu.make_async_copy(W3, u2_out.at[:, other_half], o_sem.at[3]),
    ]
    u1_copy[1].start()
    u2_copy[0].start()
    w_copy.wait_recv()
    u2_copy[1].start()
    rest = G.at[0 : nobs - 1, :]
    remote(rest, rest, g_send, g_recv, partner).wait_recv()
    sums = jnp.sum(G[...], axis=0, keepdims=True)

    norm = sums[:, 0:rows]
    cross = sums[:, rows : 2 * rows]
    image = sums[:, 2 * rows : 3 * rows]
    size = norm / cross
    norm_next = size * size * image - norm
    more = 1.0 + norm_next / (norm + EPSILON)
    curve = (more * cross - 2.0 * size * image) * more + size * size * sums[:, 3 * rows :]
    size_next = norm_next / curve
    place = lax.broadcasted_iota(jnp.int32, (LANES, rows), 0)
    table = jnp.where(place == 0, size + size_next * more, size * size_next)
    table = jnp.concatenate([table, jnp.zeros((LANES, LANES - rows), f32)], axis=1)
    c_out[...] = table.T[0:rows, :]

    for copy in [meta_copy] + a_out + relays + f_out + u_out + v_out + [e_copy, w_copy]:
        copy.wait_send()
    remote(rest, rest, g_send, g_recv, partner).wait_send()
    for copy in u1_copy + u2_copy:
        copy.wait()


def combine(start, image, again, factors, x_out, r_out):
    linear, square = factors[:, 0:1], factors[:, 1:2]
    x_out[...] = linear * start[...] - square * image[...]
    r_out[...] = start[...] - linear * image[...] + square * again[...]


def body(anomalies, innovations, obs_error, positions, pair_far, block, nx):
    f32, bf16 = jnp.float32, jnp.bfloat16
    rows, width = anomalies.shape
    nobs, nmem = lax.axis_size("obs"), lax.axis_size("mem")
    half, rows2, members = 2 * block, 2 * rows, rows * nmem
    vmem = pl.BlockSpec(memory_space=pltpu.VMEM)
    whole = pl.BlockSpec(memory_space=pl.ANY)
    dma = pltpu.SemaphoreType.DMA
    scratch = [
        pltpu.VMEM((3, members, half), bf16),
        pltpu.VMEM((3 * half, members), bf16),
        pltpu.VMEM((3, rows2, half), f32),
        pltpu.VMEM((3, rows2, half), f32),
        pltpu.VMEM((2 * rows2, 3 * half), bf16),
        pltpu.VMEM((2, 5 * block, block), bf16),
        pltpu.VMEM((2, 5 * block, block), bf16),
        pltpu.VMEM((2, 5 * block, block), f32),
        pltpu.VMEM((2, 3 * half, LANES), f32),
        pltpu.VMEM((3, 8, half), f32),
        pltpu.VMEM((8 * rows, LANES), f32),
        pltpu.VMEM((rows2, half), f32),
        pltpu.VMEM((rows, half), f32),
        pltpu.VMEM((2, 4 * rows), f32),
        pltpu.VMEM((1, 4 * rows), f32),
        pltpu.VMEM((nobs, 4 * rows), f32),
        dma((7,)), dma((7,)),
        dma((2, 8)), dma((2,)),
        dma((4,)), dma((4,)),
        dma, dma,
        dma((2, 2)), dma((2, 2)),
        dma, dma,
        dma, dma,
        dma, dma,
        pltpu.SemaphoreType.REGULAR((4,)),
        dma((4,)),
    ]
    image, again, factors = pl.pallas_call(
        functools.partial(kernel, block, nobs, nmem, nx),
        out_shape=[jax.ShapeDtypeStruct((rows, width), f32)] * 2 + [jax.ShapeDtypeStruct((rows, LANES), f32)],
        in_specs=[vmem] * 4 + [pl.BlockSpec(memory_space=pltpu.SMEM)],
        out_specs=[whole, whole, vmem],
        scratch_shapes=scratch,
        compiler_params=pltpu.CompilerParams(
            collective_id=0, has_side_effects=True, vmem_limit_bytes=56 * 1024 * 1024
        ),
        name="filter_steps",
    )(anomalies, innovations, obs_error[None, :], positions, pair_far)
    return tuple(
        pl.pallas_call(
            combine,
            out_shape=[jax.ShapeDtypeStruct((rows, width), f32)] * 2,
            in_specs=[vmem] * 4,
            out_specs=[vmem] * 2,
            name="combine",
        )(innovations, image, again, factors)
    )


def solution(mesh, block=B, nx=NX):
    in_specs = (P("mem", "obs"), P("mem", "obs"), P("obs"), P(None, "obs"), P("obs"))
    out_specs = (P("mem", "obs"), P("mem", "obs"))
    return jax.shard_map(
        functools.partial(body, block=block, nx=nx),
        mesh=mesh,
        in_specs=in_specs,
        out_specs=out_specs,
        check_vma=False,
    )
```

```python
import functools
import math

import jax
import jax.numpy as jnp
from jax import lax
from jax.experimental import pallas as pl
from jax.experimental.pallas import tpu as pltpu
from jax.sharding import PartitionSpec as P

B = 512
NX = 4
EPSILON = 1e-06
ROOT2 = math.sqrt(2.0)
SCALE = 48.0 * ROOT2
MESH = pl.DeviceIdType.MESH
LANES = 128
CHUNK = 32


def remote(src, dst, send, recv, device):
    return pltpu.make_async_remote_copy(
        src_ref=src, dst_ref=dst, send_sem=send, recv_sem=recv, device_id=device, device_id_type=MESH
    )


def kernel(
    block, nobs, nmem, nx,
    anom, innov, oerr, places, far, x_out, r_out,
    X, XT, U, V, UH, CH, CL, TP, PI, META, PP, W2, W3, SB, G, XO, RO,
    a_send, a_recv, f_send, f_recv, u_send, u_recv, m_send, m_recv, v_send, v_recv, w_send, w_recv,
    g_send, g_recv, reach, o_sem,
):
    f32, bf16 = jnp.float32, jnp.bfloat16
    half = 2 * block
    rows = anom.shape[0]
    rows2 = 2 * rows
    nz = nobs // nx
    o = lax.axis_index("obs")
    mm = lax.axis_index("mem")
    c = lax.rem(mm, 2)
    y2 = mm - c
    up = lax.rem(y2 + 2, nmem)
    down = lax.rem(y2 + nmem - 2, nmem)
    across_y = lax.rem(y2 + nmem // 2, nmem)
    pm = y2 + 1 - c
    z = lax.div(o, nx)
    x = lax.rem(o, nx)
    left = (lax.rem(o + nobs - 1 + c, nobs), pm)
    right = (lax.rem(o + c, nobs), pm)
    partner = (o, pm)
    far_to = (lax.rem(o + nobs + 1 - 2 * c, nobs), mm)
    far_from = (lax.rem(o + nobs - 1 + 2 * c, nobs), mm)
    off_chip = (lax.rem(o + nobs - 1 + 2 * c, nobs), pm)

    def peer(dz, dx, dc=0):
        return (lax.rem(z + dz, nz) * nx + lax.rem(x + dx, nx), pm if dc else mm)

    barrier = pltpu.get_barrier_semaphore()
    near = [partner, left, right, far_to, far_from]
    near += [(o, y + k) for y in (up, down) for k in range(2)]
    near += [(off_chip[0], y + 1 - c) for y in (up, down)]
    near += [peer(0, dx, dc) for dx in range(1, nx) for dc in range(2)]
    near += [peer(dz, 0) for dz in sorted({1, nz - 1})]
    for device in near:
        pl.semaphore_signal(barrier, inc=1, device_id=device, device_id_type=MESH)

    own_rows = pl.ds(pl.multiple_of(mm * rows, rows), rows)
    core_rows = pl.ds(pl.multiple_of(c * rows, rows), rows)
    partner_rows = pl.ds(pl.multiple_of((1 - c) * rows, rows), rows)
    own_half = pl.ds(pl.multiple_of(c * half, half), half)
    other_half = pl.ds(pl.multiple_of((1 - c) * half, half), half)
    pf = places[...].astype(f32) * ROOT2
    for h in range(2):
        flags = jnp.concatenate(
            [jnp.full((1, block), far[2 * h + b].astype(f32), f32) for b in range(2)], axis=1
        )
        META[1 - c + h] = jnp.concatenate(
            [pf[:, h * half : (h + 1) * half], flags, jnp.zeros((5, half), f32)], axis=0
        )
    X[1, own_rows, :] = anom[:, own_half]
    pl.semaphore_wait(barrier, len(near))

    steps = [step for step in (1, 2, 4, 8) if 2 * step <= nz]

    def tell(k):
        for dz in sorted({steps[k], nz - steps[k]}):
            pl.semaphore_signal(reach.at[k], inc=1, device_id=peer(dz, 0), device_id_type=MESH)

    def hear(k):
        pl.semaphore_wait(reach.at[k], len({steps[k], nz - steps[k]}))

    def widen(k):
        if k < len(steps):
            hear(k)
            if k + 1 < len(steps):
                tell(k + 1)

    meta_copy = remote(META.at[1], META.at[2 - 2 * c], m_send, m_recv, off_chip)
    meta_copy.start()
    meta_back = remote(META.at[1], META.at[2 * c], m_send, m_recv, off_chip)

    def half_of(core):
        return pl.ds(pl.multiple_of(core * half, half), half)

    def rows_of(member):
        return pl.ds(pl.multiple_of(member * rows, rows), rows)

    a_out = []
    for way, slot in ((up + c * (down - up), 1 + 3 * c), (down + c * (up - down), 3 - c)):
        for core in range(2):
            k = lax.rem(c + core, 2)
            copy = remote(
                anom.at[:, half_of(k)], X.at[1, own_rows, :], a_send.at[len(a_out) + 1], a_recv.at[slot], (o, way + k)
            )
            a_out.append(copy)
    a_out.append(remote(anom.at[:, other_half], X.at[1, own_rows, :], a_send.at[0], a_recv.at[0], partner))
    for copy in a_out:
        copy.start()

    u_out = [
        remote(innov.at[:, own_half], U.at[2, core_rows, :], u_send.at[0], u_recv.at[0], left),
        remote(innov.at[:, own_half], U.at[0, core_rows, :], u_send.at[1], u_recv.at[1], right),
        remote(innov.at[:, other_half], U.at[1, core_rows, :], u_send.at[2], u_recv.at[2], partner),
        remote(innov.at[:, other_half], U.at[2 * c, core_rows, :], u_send.at[3], u_recv.at[3], far_to),
    ]
    u_in = [
        remote(innov.at[:, own_half], U.at[2, partner_rows, :], u_send.at[0], u_recv.at[0], left),
        remote(innov.at[:, own_half], U.at[0, partner_rows, :], u_send.at[1], u_recv.at[1], right),
        remote(innov.at[:, other_half], U.at[1, partner_rows, :], u_send.at[2], u_recv.at[2], partner),
        remote(innov.at[:, other_half], U.at[2 * c, core_rows, :], u_send.at[3], u_recv.at[3], far_to),
    ]

    sources = [mm, pm, down, down + 1, up, up + 1, across_y, across_y + 1]
    f_out, relays = [], []

    def arrived(k):
        piece = rows_of(sources[k])
        remote(anom.at[:, own_half], X.at[1, piece, :], a_send.at[k - 1], a_recv.at[k - 1], partner).wait_recv()

    def forward(k):
        piece = rows_of(sources[k])
        if k > 0:
            arrived(k)
        if k in (2, 5):
            way = up if k == 2 else down
            slot = 5 if k == 2 else 6
            relays.append(remote(X.at[1, piece, :], X.at[1, piece, :], a_send.at[slot], a_recv.at[slot], (o, way + c)))
            relays.append(
                remote(
                    X.at[1, piece, :], X.at[2 - 2 * c, piece, :], f_send.at[0, slot + 1], f_recv.at[c],
                    (off_chip[0], way + 1 - c),
                )
            )
            relays[-2].start()
            relays[-1].start()
        if k > 5:
            f_out.append(
                remote(X.at[1, piece, :], X.at[2 * c, piece, :], f_send.at[1, k], f_recv.at[1 - c], partner)
            )
            f_out[-1].start()
            return
        one = remote(X.at[1, piece, :], X.at[2, piece, :], f_send.at[0, k], f_recv.at[0], left)
        two = remote(X.at[1, piece, :], X.at[0, piece, :], f_send.at[1, k], f_recv.at[1], right)
        one.start()
        two.start()
        f_out.extend([one, two])

    forward(0)
    for copy in u_out:
        copy.start()
    tell(0)
    for h in range(2):
        U[1 - c + h, core_rows, :] = innov[:, h * half : (h + 1) * half]

    off_side, on_side = c, 1 - c

    def span(start, size):
        return pl.ds(start if isinstance(start, int) else pl.multiple_of(start, size), size)

    def columns(slot):
        for k in range(half // LANES):
            for axis in range(2):
                line = META[slot, axis : axis + 1, k * LANES : (k + 1) * LANES]
                PI[axis, span(slot * half + k * LANES, LANES), :] = jnp.broadcast_to(line, (LANES, LANES)).T

    def taper(s, w, close):
        cols = span(s * block, block)
        shift = (w - 2 - s) * ROOT2 if isinstance(w, int) else (w - 2 - s).astype(f32) * ROOT2
        along = META[1, 0:1, cols] - shift
        across = META[1, 1:2, cols]
        times = block // LANES

        def step(k, carry):
            theirs = span(w * block + k * CHUNK, CHUNK)
            g = jnp.concatenate([PI[0, theirs, :]] * times, axis=1) - along
            h = jnp.concatenate([PI[1, theirs, :]] * times, axis=1) - across
            square = g * g + h * h
            if close:
                square = jnp.maximum(square, 1e-30)
            inverse = lax.rsqrt(square)
            y = square * inverse
            rest = jnp.maximum(2.0 * ROOT2 - y, 0.0)
            rest = rest * rest
            value = (rest * rest) * ((y - inverse) + 2.0 * ROOT2)
            if close:
                inner = (-3.0 * y + 0.125 * SCALE) * y + 0.3125 * SCALE / ROOT2
                inner = (inner * y - (5.0 / 6.0) * SCALE) * square + SCALE
                value = jnp.maximum(value, inner)
            TP[s, span((w - s) * block + k * CHUNK, CHUNK), :] = value
            return carry

        lax.fori_loop(0, block // CHUNK, step, 0, unroll=2)

    def cross_pair(side):
        return 1 - side, 1 + 3 * side

    def next_pair(side):
        return side, 1 + 3 * side

    def outer_pair(side):
        return side, 5 * side

    columns(1)
    taper(0, 2, True)
    columns(2 * on_side)
    taper(0, 3, True)
    forward(1)
    taper(1, 3, True)
    taper(*next_pair(on_side), True)
    forward(2)
    taper(*cross_pair(on_side), False)
    forward(5)
    taper(*outer_pair(on_side), False)
    forward(3)
    forward(4)
    widen(0)
    meta_back.wait_recv()
    columns(2 * off_side)
    taper(*cross_pair(off_side), False)
    taper(*next_pair(off_side), True)
    forward(6)
    taper(*outer_pair(off_side), False)
    forward(7)
    widen(1)

    def turn(slot):
        part = 2 * LANES
        for k in range(half // part):
            XT[span(slot * half + k * part, part), :] = X[slot, :, k * part : (k + 1) * part].T

    def couple(s, w, factor=None):
        at = span((w - s) * block, block)
        value = jnp.dot(
            XT[span(w * block, block), :], X[1, :, span(s * block, block)], preferred_element_type=f32
        ) * TP[s, at, :]
        if factor is not None:
            value = value * factor
        high = value.astype(bf16)
        CH[s, at, :] = high
        CL[s, at, :] = (value - high.astype(f32)).astype(bf16)

    def present(side):
        chain = 2 * o + c
        edge = jnp.where(side == 0, 0, 2 * nobs - 1)
        return jnp.where(chain == edge, 0.0, 1.0).astype(f32)

    def listed(s, side):
        return META[side, 2:3, span(s * block, block)] * present(side)

    def split(values, slot):
        cols = span(slot * half, half)
        high = values.astype(bf16)
        UH[0:rows2, cols] = high
        UH[rows2 : 2 * rows2, cols] = (values - high.astype(f32)).astype(bf16)

    factor = 1.0 / (SCALE * (rows * nmem - 1))

    def multiply(s, first_row, first_block, count):
        cols = span(first_block * block, count * block) if isinstance(first_block, int) else pl.ds(
            pl.multiple_of(first_block * block, block), count * block
        )
        at = pl.ds(pl.multiple_of(first_row * block, block), count * block)
        full = jnp.dot(UH[:, cols], CH[s, at, :], preferred_element_type=f32)
        low = jnp.dot(UH[0:rows2, cols], CL[s, at, :], preferred_element_type=f32)
        return (full[0:rows2] + full[rows2:] + low) * factor

    def own_product(s):
        if s == 0:
            return multiply(0, 2, 2, 2)
        cols = slice(2 * block, 3 * block)
        at = slice(3 * block, 4 * block)
        turned = (((1,), (1,)), ((), ()))
        full = lax.dot_general(UH[:, cols], CH[0, at, :], turned, preferred_element_type=f32)
        low = lax.dot_general(UH[0:rows2, cols], CL[0, at, :], turned, preferred_element_type=f32)
        return multiply(1, 2, 3, 1) + (full[0:rows2] + full[rows2:] + low) * factor

    def cross_product(side):
        return multiply(1 - side, 4 * side, 1 + 3 * side, 1)

    def side_product(side):
        return multiply(side, 3 * side, 4 * side, 2)

    def noise(s):
        return oerr[:, pl.ds(pl.multiple_of(c * half + s * block, block), block)]

    def wait_anomalies(side):
        remote(X.at[1], X.at[2 * side], f_send.at[0, 0], f_recv.at[1 - side], partner).wait_recv()

    def couple_cross(side):
        s, w = cross_pair(side)
        couple(s, w, listed(s, side))

    def couple_side(side):
        couple(*next_pair(side), present(side))
        s, w = outer_pair(side)
        couple(s, w, listed(s, side))

    turn(1)
    for s, w in ((0, 2), (0, 3), (1, 3)):
        couple(s, w)
    u_in[2].wait_recv()
    split(U[1], 1)
    for s in range(2):
        cols = slice(s * block, (s + 1) * block)
        V[1, :, cols] = U[1, :, cols] * noise(s) + own_product(s)
    remote(innov.at[:, own_half], U.at[2 * on_side, partner_rows, :], u_send.at[0], u_recv.at[1 - on_side], partner).wait_recv()
    split(U[2 * on_side], 2 * on_side)
    wait_anomalies(on_side)
    turn(2 * on_side)
    couple_cross(on_side)
    couple_side(on_side)
    V[1, :, span((1 - on_side) * block, block)] += cross_product(on_side)
    V[1, :, span(on_side * block, block)] += side_product(on_side)
    widen(2)
    remote(innov.at[:, own_half], U.at[2 * off_side, partner_rows, :], u_send.at[0], u_recv.at[1 - off_side], partner).wait_recv()
    u_in[3].wait_recv()
    split(U[2 * off_side], 2 * off_side)
    wait_anomalies(off_side)
    turn(2 * off_side)

    v_out = []

    def send_image(s, part):
        cols = span(s * block, block)
        v_out.append(remote(V.at[1, :, cols], V.at[2, :, cols], v_send.at[0, part], v_recv.at[0, part], left))
        v_out.append(remote(V.at[1, :, cols], V.at[0, :, cols], v_send.at[1, part], v_recv.at[1, part], right))
        v_out[-2].start()
        v_out[-1].start()

    couple_cross(off_side)
    V[1, :, span((1 - off_side) * block, block)] += cross_product(off_side)
    send_image(1 - off_side, 0)
    couple_side(off_side)
    V[1, :, span(off_side * block, block)] += side_product(off_side)
    send_image(off_side, 1)

    def lane_sums(d, value):
        total = value[:, 0:LANES]
        for k in range(1, half // LANES):
            total = total + value[:, k * LANES : (k + 1) * LANES]
        if d == 3:
            return jnp.sum(total.T, axis=0, keepdims=True)
        for h in range(2):
            PP[(3 * h + d) * rows : (3 * h + d + 1) * rows, :] = total[h * rows : (h + 1) * rows]

    def wait_image(side):
        for part in range(2):
            s = c if part == 0 else 1 - c
            cols = span(s * block, block)
            remote(
                V.at[1, :, cols], V.at[2 * side, :, cols], v_send.at[0, part], v_recv.at[1 - side, part], partner
            ).wait_recv()
        split(V[2 * side], 2 * side)

    split(V[1], 1)
    for s in range(2):
        cols = slice(s * block, (s + 1) * block)
        W2[:, cols] = V[1, :, cols] * noise(s) + own_product(s)
    lane_sums(0, U[1] * U[1])
    lane_sums(1, U[1] * V[1])
    lane_sums(2, V[1] * V[1])
    early = jnp.sum(PP[0 : 3 * rows2, :].T, axis=0, keepdims=True)
    wait_image(on_side)
    W2[:, span((1 - on_side) * block, block)] += cross_product(on_side)
    W2[:, span(on_side * block, block)] += side_product(on_side)
    widen(3)
    wait_image(off_side)
    W2[:, span((1 - off_side) * block, block)] += cross_product(off_side)
    W2[:, span(off_side * block, block)] += side_product(off_side)

    late = lane_sums(3, V[1] * W2[...])
    for h in range(2):
        SB[h : h + 1, :] = jnp.concatenate(
            [early[:, 3 * h * rows : 3 * (h + 1) * rows], late[:, h * rows : (h + 1) * rows]], axis=1
        )
    mine = pl.ds(2 * o + c, 1)
    G[mine, :] = SB[pl.ds(c, 1), :]
    offsets = [(dz, dx, dc) for dz in range(nz) for dx in range(nx) for dc in range(2) if dz or dx or dc]
    offsets.sort(key=lambda d: -(min(d[0], nz - d[0]) + min(d[1], nx - d[1])))
    for dz, dx, dc in offsets:
        which = 1 - c if dc else c
        remote(SB.at[pl.ds(which, 1), :], G.at[mine, :], g_send, g_recv, peer(dz, dx, dc)).start()
    w_copy = remote(W2.at[partner_rows, :], W3, w_send, w_recv, partner)
    w_copy.start()
    w_copy.wait_recv()
    rest = G.at[0 : 2 * nobs - 1, :]
    remote(rest, rest, g_send, g_recv, partner).wait_recv()
    sums = jnp.sum(G[...], axis=0, keepdims=True)

    norm = sums[:, 0:rows]
    cross = sums[:, rows : 2 * rows]
    image = sums[:, 2 * rows : 3 * rows]
    size = norm / cross
    norm_next = size * size * image - norm
    more = 1.0 + norm_next / (norm + EPSILON)
    curve = (more * cross - 2.0 * size * image) * more + size * size * sums[:, 3 * rows :]
    size_next = norm_next / curve
    place = lax.broadcasted_iota(jnp.int32, (LANES, rows), 0)
    table = jnp.where(place == 0, size + size_next * more, size * size_next)
    table = jnp.concatenate([table, jnp.zeros((LANES, LANES - rows), f32)], axis=1)
    PP[0:LANES, :] = table.T
    linear, square = PP[0:rows, 0:1], PP[0:rows, 1:2]
    o_copy = []
    for k, (where, image, again) in enumerate(
        ((own_half, V[1, core_rows, :], W2[core_rows, :]), (other_half, V[2 - 2 * c, core_rows, :], W3[...]))
    ):
        start = innov[:, where]
        XO[:, where] = linear * start - square * image
        RO[:, where] = start - linear * image + square * again
        for n, (result, out) in enumerate(((XO, x_out), (RO, r_out))):
            o_copy.append(pltpu.make_async_copy(result.at[:, where], out.at[:, where], o_sem.at[2 * k + n]))
            o_copy[-1].start()

    for copy in [meta_copy] + a_out + relays + f_out + u_out + v_out + [w_copy]:
        copy.wait_send()
    remote(rest, rest, g_send, g_recv, partner).wait_send()
    for copy in o_copy:
        copy.wait()


def hand_over(x_in, r_in, x_out, r_out, sems):
    copies = []
    part = x_in.shape[0] // 4
    for n, (source, target) in enumerate(((x_in, x_out), (r_in, r_out))):
        for k in range(4):
            at = slice(k * part, (k + 1) * part)
            copies.append(pltpu.make_async_copy(source.at[at, :], target.at[at, :], sems.at[4 * n + k]))
            copies[-1].start()
    for copy in copies:
        copy.wait()


def body(anomalies, innovations, obs_error, positions, pair_far, block, nx):
    f32, bf16 = jnp.float32, jnp.bfloat16
    rows, width = anomalies.shape
    nobs, nmem = lax.axis_size("obs"), lax.axis_size("mem")
    half, rows2, members = 2 * block, 2 * rows, rows * nmem
    vmem = pl.BlockSpec(memory_space=pltpu.VMEM)
    whole = pl.BlockSpec(memory_space=pl.ANY)
    dma = pltpu.SemaphoreType.DMA
    scratch = [
        pltpu.VMEM((3, members, half), bf16),
        pltpu.VMEM((3 * half, members), bf16),
        pltpu.VMEM((3, rows2, half), f32),
        pltpu.VMEM((3, rows2, half), f32),
        pltpu.VMEM((2 * rows2, 3 * half), bf16),
        pltpu.VMEM((2, 5 * block, block), bf16),
        pltpu.VMEM((2, 5 * block, block), bf16),
        pltpu.VMEM((2, 5 * block, block), f32),
        pltpu.VMEM((2, 3 * half, LANES), f32),
        pltpu.VMEM((3, 8, half), f32),
        pltpu.VMEM((8 * rows, LANES), f32),
        pltpu.VMEM((rows2, half), f32),
        pltpu.VMEM((rows, half), f32),
        pltpu.VMEM((2, 4 * rows), f32),
        pltpu.VMEM((2 * nobs, 4 * rows), f32),
        pltpu.VMEM((rows, width), f32),
        pltpu.VMEM((rows, width), f32),
        dma((7,)), dma((7,)),
        dma((2, 8)), dma((2,)),
        dma((4,)), dma((4,)),
        dma, dma,
        dma((2, 2)), dma((2, 2)),
        dma, dma,
        dma, dma,
        pltpu.SemaphoreType.REGULAR((4,)),
        dma((4,)),
    ]
    results = pl.pallas_call(
        functools.partial(kernel, block, nobs, nmem, nx),
        out_shape=[jax.ShapeDtypeStruct((rows, width), f32)] * 2,
        in_specs=[vmem] * 4 + [pl.BlockSpec(memory_space=pltpu.SMEM)],
        out_specs=[whole] * 2,
        scratch_shapes=scratch,
        compiler_params=pltpu.CompilerParams(
            collective_id=0, has_side_effects=True, vmem_limit_bytes=56 * 1024 * 1024
        ),
        name="filter_steps",
    )(anomalies, innovations, obs_error[None, :], positions, pair_far)
    return tuple(
        pl.pallas_call(
            hand_over,
            out_shape=[jax.ShapeDtypeStruct((rows, width), f32)] * 2,
            in_specs=[whole] * 2,
            out_specs=[whole] * 2,
            scratch_shapes=[dma((8,))],
            name="hand_over",
        )(*results)
    )


def solution(mesh, block=B, nx=NX):
    in_specs = (P("mem", "obs"), P("mem", "obs"), P("obs"), P(None, "obs"), P("obs"))
    out_specs = (P("mem", "obs"), P("mem", "obs"))
    return jax.shard_map(
        functools.partial(body, block=block, nx=nx),
        mesh=mesh,
        in_specs=in_specs,
        out_specs=out_specs,
        check_vma=False,
    )
```

```python
import functools
import math

import jax
import jax.numpy as jnp
from jax import lax
from jax.experimental import pallas as pl
from jax.experimental.pallas import tpu as pltpu
from jax.sharding import PartitionSpec as P

B = 512
NX = 4
EPSILON = 1e-06
ROOT2 = math.sqrt(2.0)
SCALE = 48.0 * ROOT2
MESH = pl.DeviceIdType.MESH
LANES = 128
CHUNK = 32


def remote(src, dst, send, recv, device):
    return pltpu.make_async_remote_copy(
        src_ref=src, dst_ref=dst, send_sem=send, recv_sem=recv, device_id=device, device_id_type=MESH
    )


def kernel(
    block, nobs, nmem, nx,
    anom, innov, oerr, places, far, u1_out, u2_out, c_out,
    X, XT, U, V, UH, CH, CL, TP, PI, META, PP, W2, W3, SB, G,
    a_send, a_recv, f_send, f_recv, u_send, u_recv, m_send, m_recv, v_send, v_recv, w_send, w_recv,
    g_send, g_recv, reach, o_sem,
):
    f32, bf16 = jnp.float32, jnp.bfloat16
    half = 2 * block
    rows = anom.shape[0]
    rows2 = 2 * rows
    nz = nobs // nx
    o = lax.axis_index("obs")
    mm = lax.axis_index("mem")
    c = lax.rem(mm, 2)
    y2 = mm - c
    up = lax.rem(y2 + 2, nmem)
    down = lax.rem(y2 + nmem - 2, nmem)
    across_y = lax.rem(y2 + nmem // 2, nmem)
    pm = y2 + 1 - c
    z = lax.div(o, nx)
    x = lax.rem(o, nx)
    left = (lax.rem(o + nobs - 1 + c, nobs), pm)
    right = (lax.rem(o + c, nobs), pm)
    partner = (o, pm)
    far_to = (lax.rem(o + nobs + 1 - 2 * c, nobs), mm)
    far_from = (lax.rem(o + nobs - 1 + 2 * c, nobs), mm)
    off_chip = (lax.rem(o + nobs - 1 + 2 * c, nobs), pm)

    def peer(dz, dx, dc=0):
        return (lax.rem(z + dz, nz) * nx + lax.rem(x + dx, nx), pm if dc else mm)

    barrier = pltpu.get_barrier_semaphore()
    near = [partner, left, right, far_to, far_from]
    near += [(o, y + k) for y in (up, down) for k in range(2)]
    near += [(off_chip[0], y + 1 - c) for y in (up, down)]
    near += [peer(0, dx, dc) for dx in range(1, nx) for dc in range(2)]
    near += [peer(dz, 0) for dz in sorted({1, nz - 1})]
    for device in near:
        pl.semaphore_signal(barrier, inc=1, device_id=device, device_id_type=MESH)

    own_rows = pl.ds(pl.multiple_of(mm * rows, rows), rows)
    core_rows = pl.ds(pl.multiple_of(c * rows, rows), rows)
    partner_rows = pl.ds(pl.multiple_of((1 - c) * rows, rows), rows)
    own_half = pl.ds(pl.multiple_of(c * half, half), half)
    other_half = pl.ds(pl.multiple_of((1 - c) * half, half), half)
    pf = places[...].astype(f32) * ROOT2
    for h in range(2):
        flags = jnp.concatenate(
            [jnp.full((1, block), far[2 * h + b].astype(f32), f32) for b in range(2)], axis=1
        )
        META[1 - c + h] = jnp.concatenate(
            [pf[:, h * half : (h + 1) * half], flags, jnp.zeros((5, half), f32)], axis=0
        )
    X[1, own_rows, :] = anom[:, own_half]
    pl.semaphore_wait(barrier, len(near))

    steps = [step for step in (1, 2, 4, 8) if 2 * step <= nz]

    def tell(k):
        for dz in sorted({steps[k], nz - steps[k]}):
            pl.semaphore_signal(reach.at[k], inc=1, device_id=peer(dz, 0), device_id_type=MESH)

    def hear(k):
        pl.semaphore_wait(reach.at[k], len({steps[k], nz - steps[k]}))

    def widen(k):
        if k < len(steps):
            hear(k)
            if k + 1 < len(steps):
                tell(k + 1)

    meta_copy = remote(META.at[1], META.at[2 - 2 * c], m_send, m_recv, off_chip)
    meta_copy.start()
    meta_back = remote(META.at[1], META.at[2 * c], m_send, m_recv, off_chip)

    def half_of(core):
        return pl.ds(pl.multiple_of(core * half, half), half)

    def rows_of(member):
        return pl.ds(pl.multiple_of(member * rows, rows), rows)

    a_out = []
    for way, slot in ((up + c * (down - up), 1 + 3 * c), (down + c * (up - down), 3 - c)):
        for core in range(2):
            k = lax.rem(c + core, 2)
            copy = remote(
                anom.at[:, half_of(k)], X.at[1, own_rows, :], a_send.at[len(a_out) + 1], a_recv.at[slot], (o, way + k)
            )
            a_out.append(copy)
    a_out.append(remote(anom.at[:, other_half], X.at[1, own_rows, :], a_send.at[0], a_recv.at[0], partner))
    for copy in a_out:
        copy.start()

    u_out = [
        remote(innov.at[:, own_half], U.at[2, core_rows, :], u_send.at[0], u_recv.at[0], left),
        remote(innov.at[:, own_half], U.at[0, core_rows, :], u_send.at[1], u_recv.at[1], right),
        remote(innov.at[:, other_half], U.at[1, core_rows, :], u_send.at[2], u_recv.at[2], partner),
        remote(innov.at[:, other_half], U.at[2 * c, core_rows, :], u_send.at[3], u_recv.at[3], far_to),
    ]
    u_in = [
        remote(innov.at[:, own_half], U.at[2, partner_rows, :], u_send.at[0], u_recv.at[0], left),
        remote(innov.at[:, own_half], U.at[0, partner_rows, :], u_send.at[1], u_recv.at[1], right),
        remote(innov.at[:, other_half], U.at[1, partner_rows, :], u_send.at[2], u_recv.at[2], partner),
        remote(innov.at[:, other_half], U.at[2 * c, core_rows, :], u_send.at[3], u_recv.at[3], far_to),
    ]

    sources = [mm, pm, down, down + 1, up, up + 1, across_y, across_y + 1]
    f_out, relays = [], []

    def arrived(k):
        piece = rows_of(sources[k])
        remote(anom.at[:, own_half], X.at[1, piece, :], a_send.at[k - 1], a_recv.at[k - 1], partner).wait_recv()

    def forward(k):
        piece = rows_of(sources[k])
        if k > 0:
            arrived(k)
        if k in (2, 5):
            way = up if k == 2 else down
            slot = 5 if k == 2 else 6
            relays.append(remote(X.at[1, piece, :], X.at[1, piece, :], a_send.at[slot], a_recv.at[slot], (o, way + c)))
            relays.append(
                remote(
                    X.at[1, piece, :], X.at[2 - 2 * c, piece, :], f_send.at[0, slot + 1], f_recv.at[c],
                    (off_chip[0], way + 1 - c),
                )
            )
            relays[-2].start()
            relays[-1].start()
        if k > 5:
            f_out.append(
                remote(X.at[1, piece, :], X.at[2 * c, piece, :], f_send.at[1, k], f_recv.at[1 - c], partner)
            )
            f_out[-1].start()
            return
        one = remote(X.at[1, piece, :], X.at[2, piece, :], f_send.at[0, k], f_recv.at[0], left)
        two = remote(X.at[1, piece, :], X.at[0, piece, :], f_send.at[1, k], f_recv.at[1], right)
        one.start()
        two.start()
        f_out.extend([one, two])

    forward(0)
    for copy in u_out:
        copy.start()
    tell(0)
    for h in range(2):
        U[1 - c + h, core_rows, :] = innov[:, h * half : (h + 1) * half]

    off_side, on_side = c, 1 - c

    def span(start, size):
        return pl.ds(start if isinstance(start, int) else pl.multiple_of(start, min(size, 2 * LANES)), size)

    def columns(slot):
        for k in range(half // LANES):
            for axis in range(2):
                line = META[slot, axis : axis + 1, k * LANES : (k + 1) * LANES]
                PI[axis, span(slot * half + k * LANES, LANES), :] = jnp.broadcast_to(line, (LANES, LANES)).T

    def taper(s, w, close):
        cols = span(s * block, block)
        shift = (w - 2 - s) * ROOT2 if isinstance(w, int) else (w - 2 - s).astype(f32) * ROOT2
        along = META[1, 0:1, cols] - shift
        across = META[1, 1:2, cols]
        times = block // LANES

        def step(k, carry):
            theirs = span(w * block + k * CHUNK, CHUNK)
            g = jnp.concatenate([PI[0, theirs, :]] * times, axis=1) - along
            h = jnp.concatenate([PI[1, theirs, :]] * times, axis=1) - across
            square = g * g + h * h
            if close:
                square = jnp.maximum(square, 1e-30)
            inverse = lax.rsqrt(square)
            y = square * inverse
            rest = jnp.maximum(2.0 * ROOT2 - y, 0.0)
            rest = rest * rest
            value = (rest * rest) * ((y - inverse) + 2.0 * ROOT2)
            if close:
                inner = (-3.0 * y + 0.125 * SCALE) * y + 0.3125 * SCALE / ROOT2
                inner = (inner * y - (5.0 / 6.0) * SCALE) * square + SCALE
                value = jnp.maximum(value, inner)
            TP[s, span((w - s) * block + k * CHUNK, CHUNK), :] = value
            return carry

        lax.fori_loop(0, block // CHUNK, step, 0, unroll=2)

    def cross_pair(side):
        return 1 - side, 1 + 3 * side

    def next_pair(side):
        return side, 1 + 3 * side

    def outer_pair(side):
        return side, 5 * side

    columns(1)
    taper(0, 2, True)
    columns(2 * on_side)
    taper(0, 3, True)
    forward(1)
    taper(1, 3, True)
    taper(*next_pair(on_side), True)
    forward(2)
    taper(*cross_pair(on_side), False)
    forward(5)
    taper(*outer_pair(on_side), False)
    forward(3)
    forward(4)
    widen(0)
    meta_back.wait_recv()
    columns(2 * off_side)
    taper(*cross_pair(off_side), False)
    taper(*next_pair(off_side), True)
    forward(6)
    taper(*outer_pair(off_side), False)
    forward(7)
    widen(1)

    def turn(slot):
        part = 2 * LANES
        for k in range(half // part):
            XT[span(slot * half + k * part, part), :] = X[slot, :, k * part : (k + 1) * part].T

    def couple(s, w, factor=None, part=slice(0, block)):
        at = span((w - s) * block, block)
        size = part.stop - part.start
        value = jnp.dot(
            XT[span(w * block, block), :], X[1, :, span(s * block + part.start, size)], preferred_element_type=f32
        ) * TP[s, at, part]
        if factor is not None:
            value = value * factor[:, part]
        high = value.astype(bf16)
        CH[s, at, part] = high
        CL[s, at, part] = (value - high.astype(f32)).astype(bf16)

    def present(side):
        chain = 2 * o + c
        edge = jnp.where(side == 0, 0, 2 * nobs - 1)
        return jnp.where(chain == edge, 0.0, 1.0).astype(f32)

    def listed(s, side):
        return META[side, 2:3, span(s * block, block)] * present(side)

    def split(values, slot):
        cols = span(slot * half, half)
        high = values.astype(bf16)
        UH[0:rows2, cols] = high
        UH[rows2 : 2 * rows2, cols] = (values - high.astype(f32)).astype(bf16)

    factor = 1.0 / (SCALE * (rows * nmem - 1))

    def multiply(s, first_row, first_block, count, part=slice(0, block)):
        cols = span(first_block * block, count * block) if isinstance(first_block, int) else pl.ds(
            pl.multiple_of(first_block * block, block), count * block
        )
        at = pl.ds(pl.multiple_of(first_row * block, block), count * block)
        full = jnp.dot(UH[:, cols], CH[s, at, part], preferred_element_type=f32)
        low = jnp.dot(UH[0:rows2, cols], CL[s, at, part], preferred_element_type=f32)
        return (full[0:rows2] + full[rows2:] + low) * factor

    def own_product(s):
        if s == 0:
            return multiply(0, 2, 2, 2)
        cols = slice(2 * block, 3 * block)
        at = slice(3 * block, 4 * block)
        turned = (((1,), (1,)), ((), ()))
        full = lax.dot_general(UH[:, cols], CH[0, at, :], turned, preferred_element_type=f32)
        low = lax.dot_general(UH[0:rows2, cols], CL[0, at, :], turned, preferred_element_type=f32)
        return multiply(1, 2, 3, 1) + (full[0:rows2] + full[rows2:] + low) * factor

    def cross_product(side, part=slice(0, block)):
        return multiply(1 - side, 4 * side, 1 + 3 * side, 1, part)

    def side_product(side, part=slice(0, block)):
        return multiply(side, 3 * side, 4 * side, 2, part)

    def noise(s):
        return oerr[:, pl.ds(pl.multiple_of(c * half + s * block, block), block)]

    def wait_anomalies(side):
        remote(X.at[1], X.at[2 * side], f_send.at[0, 0], f_recv.at[1 - side], partner).wait_recv()

    def couple_cross(side, part=slice(0, block)):
        s, w = cross_pair(side)
        couple(s, w, listed(s, side), part)

    def couple_side(side, part=slice(0, block)):
        couple(*next_pair(side), jnp.full((1, block), 1.0, f32) * present(side), part)
        s, w = outer_pair(side)
        couple(s, w, listed(s, side), part)

    turn(1)
    for s, w in ((0, 2), (0, 3), (1, 3)):
        couple(s, w)
    u_in[2].wait_recv()
    split(U[1], 1)
    for s in range(2):
        cols = slice(s * block, (s + 1) * block)
        V[1, :, cols] = U[1, :, cols] * noise(s) + own_product(s)
    remote(innov.at[:, own_half], U.at[2 * on_side, partner_rows, :], u_send.at[0], u_recv.at[1 - on_side], partner).wait_recv()
    split(U[2 * on_side], 2 * on_side)
    wait_anomalies(on_side)
    turn(2 * on_side)
    couple_cross(on_side)
    couple_side(on_side)
    V[1, :, span((1 - on_side) * block, block)] += cross_product(on_side)
    V[1, :, span(on_side * block, block)] += side_product(on_side)
    widen(2)
    remote(innov.at[:, own_half], U.at[2 * off_side, partner_rows, :], u_send.at[0], u_recv.at[1 - off_side], partner).wait_recv()
    u_in[3].wait_recv()
    split(U[2 * off_side], 2 * off_side)
    wait_anomalies(off_side)
    turn(2 * off_side)

    v_out = []

    quarter = block // 2
    halves = [slice(0, quarter), slice(quarter, block)]

    def send_image(s, k):
        cols = span(s * block + halves[k % 2].start, quarter)
        v_out.append(remote(V.at[1, :, cols], V.at[2, :, cols], v_send.at[0, k], v_recv.at[0, k], left))
        v_out.append(remote(V.at[1, :, cols], V.at[0, :, cols], v_send.at[1, k], v_recv.at[1, k], right))
        v_out[-2].start()
        v_out[-1].start()

    for k, part in enumerate(halves):
        couple_cross(off_side, part)
        V[1, :, span((1 - off_side) * block + part.start, quarter)] += cross_product(off_side, part)
        send_image(1 - off_side, k)
    for k, part in enumerate(halves):
        couple_side(off_side, part)
        V[1, :, span(off_side * block + part.start, quarter)] += side_product(off_side, part)
        send_image(off_side, 2 + k)

    o_copy = [pltpu.make_async_copy(V.at[1, core_rows, :], u1_out.at[:, own_half], o_sem.at[0])]
    o_copy[0].start()

    def lane_sums(d, value):
        total = value[:, 0:LANES]
        for k in range(1, half // LANES):
            total = total + value[:, k * LANES : (k + 1) * LANES]
        if d == 3:
            return jnp.sum(total.T, axis=0, keepdims=True)
        for h in range(2):
            PP[(3 * h + d) * rows : (3 * h + d + 1) * rows, :] = total[h * rows : (h + 1) * rows]

    def wait_image(side):
        for k in range(4):
            s = c if k < 2 else 1 - c
            cols = span(s * block + halves[k % 2].start, quarter)
            remote(
                V.at[1, :, cols], V.at[2 * side, :, cols], v_send.at[0, k], v_recv.at[1 - side, k], partner
            ).wait_recv()
        split(V[2 * side], 2 * side)

    split(V[1], 1)
    for s in range(2):
        cols = slice(s * block, (s + 1) * block)
        W2[:, cols] = V[1, :, cols] * noise(s) + own_product(s)
    lane_sums(0, U[1] * U[1])
    lane_sums(1, U[1] * V[1])
    lane_sums(2, V[1] * V[1])
    early = jnp.sum(PP[0 : 3 * rows2, :].T, axis=0, keepdims=True)
    wait_image(on_side)
    o_copy.append(pltpu.make_async_copy(V.at[2 * on_side, core_rows, :], u1_out.at[:, other_half], o_sem.at[1]))
    o_copy[1].start()
    W2[:, span((1 - on_side) * block, block)] += cross_product(on_side)
    W2[:, span(on_side * block, block)] += side_product(on_side)
    widen(3)
    wait_image(off_side)
    W2[:, span((1 - off_side) * block, block)] += cross_product(off_side)
    W2[:, span(off_side * block, block)] += side_product(off_side)

    late = lane_sums(3, V[1] * W2[...])
    for h in range(2):
        SB[h : h + 1, :] = jnp.concatenate(
            [early[:, 3 * h * rows : 3 * (h + 1) * rows], late[:, h * rows : (h + 1) * rows]], axis=1
        )
    mine = pl.ds(2 * o + c, 1)
    G[mine, :] = SB[pl.ds(c, 1), :]
    offsets = [(dz, dx, dc) for dz in range(nz) for dx in range(nx) for dc in range(2) if dz or dx or dc]
    offsets.sort(key=lambda d: -(min(d[0], nz - d[0]) + min(d[1], nx - d[1])))
    for dz, dx, dc in offsets:
        which = 1 - c if dc else c
        remote(SB.at[pl.ds(which, 1), :], G.at[mine, :], g_send, g_recv, peer(dz, dx, dc)).start()
    w_copy = remote(W2.at[partner_rows, :], W3, w_send, w_recv, partner)
    w_copy.start()
    o_copy.append(pltpu.make_async_copy(W2.at[core_rows, :], u2_out.at[:, own_half], o_sem.at[2]))
    o_copy[2].start()
    w_copy.wait_recv()
    o_copy.append(pltpu.make_async_copy(W3, u2_out.at[:, other_half], o_sem.at[3]))
    o_copy[3].start()
    rest = G.at[0 : 2 * nobs - 1, :]
    remote(rest, rest, g_send, g_recv, partner).wait_recv()
    sums = jnp.sum(G[...], axis=0, keepdims=True)

    norm = sums[:, 0:rows]
    cross = sums[:, rows : 2 * rows]
    image = sums[:, 2 * rows : 3 * rows]
    size = norm / cross
    norm_next = size * size * image - norm
    more = 1.0 + norm_next / (norm + EPSILON)
    curve = (more * cross - 2.0 * size * image) * more + size * size * sums[:, 3 * rows :]
    size_next = norm_next / curve
    place = lax.broadcasted_iota(jnp.int32, (LANES, rows), 0)
    table = jnp.where(place == 0, size + size_next * more, size * size_next)
    table = jnp.concatenate([table, jnp.zeros((LANES, LANES - rows), f32)], axis=1)
    c_out[...] = table.T[0:rows, :]

    for copy in [meta_copy] + a_out + relays + f_out + u_out + v_out + [w_copy]:
        copy.wait_send()
    remote(rest, rest, g_send, g_recv, partner).wait_send()
    for copy in o_copy:
        copy.wait()


def combine(start, image, again, factors, x_out, r_out):
    linear, square = factors[:, 0:1], factors[:, 1:2]
    x_out[...] = linear * start[...] - square * image[...]
    r_out[...] = start[...] - linear * image[...] + square * again[...]


def body(anomalies, innovations, obs_error, positions, pair_far, block, nx):
    f32, bf16 = jnp.float32, jnp.bfloat16
    rows, width = anomalies.shape
    nobs, nmem = lax.axis_size("obs"), lax.axis_size("mem")
    half, rows2, members = 2 * block, 2 * rows, rows * nmem
    vmem = pl.BlockSpec(memory_space=pltpu.VMEM)
    whole = pl.BlockSpec(memory_space=pl.ANY)
    dma = pltpu.SemaphoreType.DMA
    scratch = [
        pltpu.VMEM((3, members, half), bf16),
        pltpu.VMEM((3 * half, members), bf16),
        pltpu.VMEM((3, rows2, half), f32),
        pltpu.VMEM((3, rows2, half), f32),
        pltpu.VMEM((2 * rows2, 3 * half), bf16),
        pltpu.VMEM((2, 5 * block, block), bf16),
        pltpu.VMEM((2, 5 * block, block), bf16),
        pltpu.VMEM((2, 5 * block, block), f32),
        pltpu.VMEM((2, 3 * half, LANES), f32),
        pltpu.VMEM((3, 8, half), f32),
        pltpu.VMEM((8 * rows, LANES), f32),
        pltpu.VMEM((rows2, half), f32),
        pltpu.VMEM((rows, half), f32),
        pltpu.VMEM((2, 4 * rows), f32),
        pltpu.VMEM((2 * nobs, 4 * rows), f32),
        dma((7,)), dma((7,)),
        dma((2, 8)), dma((2,)),
        dma((4,)), dma((4,)),
        dma, dma,
        dma((2, 4)), dma((2, 4)),
        dma, dma,
        dma, dma,
        pltpu.SemaphoreType.REGULAR((4,)),
        dma((4,)),
    ]
    image, again, factors = pl.pallas_call(
        functools.partial(kernel, block, nobs, nmem, nx),
        out_shape=[jax.ShapeDtypeStruct((rows, width), f32)] * 2 + [jax.ShapeDtypeStruct((rows, LANES), f32)],
        in_specs=[vmem] * 4 + [pl.BlockSpec(memory_space=pltpu.SMEM)],
        out_specs=[whole, whole, vmem],
        scratch_shapes=scratch,
        compiler_params=pltpu.CompilerParams(
            collective_id=0, has_side_effects=True, vmem_limit_bytes=56 * 1024 * 1024
        ),
        name="filter_steps",
    )(anomalies, innovations, obs_error[None, :], positions, pair_far)
    return tuple(
        pl.pallas_call(
            combine,
            out_shape=[jax.ShapeDtypeStruct((rows, width), f32)] * 2,
            in_specs=[vmem] * 4,
            out_specs=[vmem] * 2,
            name="combine",
        )(innovations, image, again, factors)
    )


def solution(mesh, block=B, nx=NX):
    in_specs = (P("mem", "obs"), P("mem", "obs"), P("obs"), P(None, "obs"), P("obs"))
    out_specs = (P("mem", "obs"), P("mem", "obs"))
    return jax.shard_map(
        functools.partial(body, block=block, nx=nx),
        mesh=mesh,
        in_specs=in_specs,
        out_specs=out_specs,
        check_vma=False,
    )
```

```python
import functools
import math

import jax
import jax.numpy as jnp
from jax import lax
from jax.experimental import pallas as pl
from jax.experimental.pallas import tpu as pltpu
from jax.sharding import PartitionSpec as P

B = 512
NX = 4
EPSILON = 1e-06
ROOT2 = math.sqrt(2.0)
SCALE = 48.0 * ROOT2
MESH = pl.DeviceIdType.MESH
LANES = 128
CHUNK = 32


def remote(src, dst, send, recv, device):
    return pltpu.make_async_remote_copy(
        src_ref=src, dst_ref=dst, send_sem=send, recv_sem=recv, device_id=device, device_id_type=MESH
    )


def kernel(
    block, nobs, nmem, nx,
    anom, innov, oerr, places, far, u1_out, u2_out, c_out,
    X, XT, U, V, UH, CH, CL, TP, PI, META, PP, W2, W3, SB, SR, G,
    a_send, a_recv, f_send, f_recv, u_send, u_recv, m_send, m_recv, v_send, v_recv, w_send, w_recv,
    e_send, e_recv, g_send, g_recv, reach, o_sem,
):
    f32, bf16 = jnp.float32, jnp.bfloat16
    half = 2 * block
    rows = anom.shape[0]
    rows2 = 2 * rows
    nz = nobs // nx
    o = lax.axis_index("obs")
    mm = lax.axis_index("mem")
    c = lax.rem(mm, 2)
    y2 = mm - c
    up = lax.rem(y2 + 2, nmem)
    down = lax.rem(y2 + nmem - 2, nmem)
    across_y = lax.rem(y2 + nmem // 2, nmem)
    pm = y2 + 1 - c
    z = lax.div(o, nx)
    x = lax.rem(o, nx)
    left = (lax.rem(o + nobs - 1 + c, nobs), pm)
    right = (lax.rem(o + c, nobs), pm)
    partner = (o, pm)
    far_to = (lax.rem(o + nobs + 1 - 2 * c, nobs), mm)
    far_from = (lax.rem(o + nobs - 1 + 2 * c, nobs), mm)
    off_chip = (lax.rem(o + nobs - 1 + 2 * c, nobs), pm)

    def peer(dz, dx):
        return (lax.rem(z + dz + nz, nz) * nx + lax.rem(x + dx + nx, nx), mm)

    barrier = pltpu.get_barrier_semaphore()
    near = [partner, left, right, far_to, far_from]
    near += [(o, y + k) for y in (up, down) for k in range(2)]
    near += [peer(0, dx) for dx in range(1, nx)]
    near += [peer(dz, 0) for dz in sorted({1, nz - 1})]
    for device in near:
        pl.semaphore_signal(barrier, inc=1, device_id=device, device_id_type=MESH)

    own_rows = pl.ds(pl.multiple_of(mm * rows, rows), rows)
    core_rows = pl.ds(pl.multiple_of(c * rows, rows), rows)
    partner_rows = pl.ds(pl.multiple_of((1 - c) * rows, rows), rows)
    own_half = pl.ds(pl.multiple_of(c * half, half), half)
    other_half = pl.ds(pl.multiple_of((1 - c) * half, half), half)
    pf = places[...].astype(f32) * ROOT2
    for h in range(2):
        flags = jnp.concatenate(
            [jnp.full((1, block), far[2 * h + b].astype(f32), f32) for b in range(2)], axis=1
        )
        META[1 - c + h] = jnp.concatenate(
            [pf[:, h * half : (h + 1) * half], flags, jnp.zeros((5, half), f32)], axis=0
        )
    X[1, own_rows, :] = anom[:, own_half]
    off_side, on_side = c, 1 - c

    def span(start, size):
        return pl.ds(start if isinstance(start, int) else pl.multiple_of(start, size), size)

    def columns(slot):
        for k in range(half // LANES):
            for axis in range(2):
                line = META[slot, axis : axis + 1, k * LANES : (k + 1) * LANES]
                PI[axis, span(slot * half + k * LANES, LANES), :] = jnp.broadcast_to(line, (LANES, LANES)).T

    def taper(s, w, close):
        cols = span(s * block, block)
        shift = (w - 2 - s) * ROOT2 if isinstance(w, int) else (w - 2 - s).astype(f32) * ROOT2
        along = META[1, 0:1, cols] - shift
        across = META[1, 1:2, cols]
        times = block // LANES

        def step(k, carry):
            theirs = span(w * block + k * CHUNK, CHUNK)
            g = jnp.concatenate([PI[0, theirs, :]] * times, axis=1) - along
            h = jnp.concatenate([PI[1, theirs, :]] * times, axis=1) - across
            square = g * g + h * h
            if close:
                square = jnp.maximum(square, 1e-30)
            inverse = lax.rsqrt(square)
            y = square * inverse
            rest = jnp.maximum(2.0 * ROOT2 - y, 0.0)
            rest = rest * rest
            value = (rest * rest) * ((y - inverse) + 2.0 * ROOT2)
            if close:
                inner = (-3.0 * y + 0.125 * SCALE) * y + 0.3125 * SCALE / ROOT2
                inner = (inner * y - (5.0 / 6.0) * SCALE) * square + SCALE
                value = jnp.maximum(value, inner)
            TP[s, span((w - s) * block + k * CHUNK, CHUNK), :] = value
            return carry

        lax.fori_loop(0, block // CHUNK, step, 0, unroll=2)

    def cross_pair(side):
        return 1 - side, 1 + 3 * side

    def next_pair(side):
        return side, 1 + 3 * side

    def outer_pair(side):
        return side, 5 * side

    columns(1)
    taper(0, 2, True)
    pl.semaphore_wait(barrier, len(near))

    steps = [step for step in (1, 2, 4, 8) if 2 * step <= nz]

    def tell(k):
        for dz in sorted({steps[k], nz - steps[k]}):
            pl.semaphore_signal(reach.at[k], inc=1, device_id=peer(dz, 0), device_id_type=MESH)

    def hear(k):
        pl.semaphore_wait(reach.at[k], len({steps[k], nz - steps[k]}))

    def widen(k):
        if k < len(steps):
            hear(k)
            if k + 1 < len(steps):
                tell(k + 1)

    meta_copy = remote(META.at[1], META.at[2 - 2 * c], m_send, m_recv, off_chip)
    meta_copy.start()
    meta_back = remote(META.at[1], META.at[2 * c], m_send, m_recv, off_chip)

    def half_of(core):
        return pl.ds(pl.multiple_of(core * half, half), half)

    def rows_of(member):
        return pl.ds(pl.multiple_of(member * rows, rows), rows)

    a_out = []
    for way, slot in ((up + c * (down - up), 1 + 3 * c), (down + c * (up - down), 3 - c)):
        for core in range(2):
            k = lax.rem(c + core, 2)
            copy = remote(
                anom.at[:, half_of(k)], X.at[1, own_rows, :], a_send.at[len(a_out) + 1], a_recv.at[slot], (o, way + k)
            )
            a_out.append(copy)
    a_out.append(remote(anom.at[:, other_half], X.at[1, own_rows, :], a_send.at[0], a_recv.at[0], partner))
    for copy in a_out:
        copy.start()

    u_out = [
        remote(innov.at[:, own_half], U.at[2, core_rows, :], u_send.at[0], u_recv.at[0], left),
        remote(innov.at[:, own_half], U.at[0, core_rows, :], u_send.at[1], u_recv.at[1], right),
        remote(innov.at[:, other_half], U.at[1, core_rows, :], u_send.at[2], u_recv.at[2], partner),
        remote(innov.at[:, other_half], U.at[2 * c, core_rows, :], u_send.at[3], u_recv.at[3], far_to),
    ]
    u_in = [
        remote(innov.at[:, own_half], U.at[2, partner_rows, :], u_send.at[0], u_recv.at[0], left),
        remote(innov.at[:, own_half], U.at[0, partner_rows, :], u_send.at[1], u_recv.at[1], right),
        remote(innov.at[:, other_half], U.at[1, partner_rows, :], u_send.at[2], u_recv.at[2], partner),
        remote(innov.at[:, other_half], U.at[2 * c, core_rows, :], u_send.at[3], u_recv.at[3], far_to),
    ]

    sources = [mm, pm, down, down + 1, up, up + 1, across_y, across_y + 1]
    f_out, relays = [], []

    def arrived(k):
        piece = rows_of(sources[k])
        remote(anom.at[:, own_half], X.at[1, piece, :], a_send.at[k - 1], a_recv.at[k - 1], partner).wait_recv()

    def forward(k):
        piece = rows_of(sources[k])
        if k > 0:
            arrived(k)
        if k == 2:
            relays.append(remote(X.at[1, piece, :], X.at[1, piece, :], a_send.at[5], a_recv.at[5], (o, up + c)))
            relays[-1].start()
        if k == 5:
            relays.append(remote(X.at[1, piece, :], X.at[1, piece, :], a_send.at[6], a_recv.at[6], (o, down + c)))
            relays[-1].start()
        one = remote(X.at[1, piece, :], X.at[2, piece, :], f_send.at[0, k], f_recv.at[0], left)
        two = remote(X.at[1, piece, :], X.at[0, piece, :], f_send.at[1, k], f_recv.at[1], right)
        one.start()
        two.start()
        f_out.extend([one, two])

    forward(0)
    for copy in u_out:
        copy.start()
    tell(0)
    for h in range(2):
        U[1 - c + h, core_rows, :] = innov[:, h * half : (h + 1) * half]

    columns(2 * on_side)
    taper(0, 3, True)
    forward(1)
    taper(1, 3, True)
    taper(*next_pair(on_side), True)
    forward(2)
    taper(*cross_pair(on_side), False)
    forward(5)
    taper(*outer_pair(on_side), False)
    forward(3)
    forward(4)
    widen(0)
    meta_back.wait_recv()
    columns(2 * off_side)
    taper(*cross_pair(off_side), False)
    taper(*next_pair(off_side), True)
    forward(6)
    taper(*outer_pair(off_side), False)
    forward(7)
    widen(1)

    def turn(slot):
        part = 2 * LANES
        for k in range(half // part):
            XT[span(slot * half + k * part, part), :] = X[slot, :, k * part : (k + 1) * part].T

    def couple(s, w, factor=None):
        at = span((w - s) * block, block)
        value = jnp.dot(
            XT[span(w * block, block), :], X[1, :, span(s * block, block)], preferred_element_type=f32
        ) * TP[s, at, :]
        if factor is not None:
            value = value * factor
        high = value.astype(bf16)
        CH[s, at, :] = high
        CL[s, at, :] = (value - high.astype(f32)).astype(bf16)

    def present(side):
        chain = 2 * o + c
        edge = jnp.where(side == 0, 0, 2 * nobs - 1)
        return jnp.where(chain == edge, 0.0, 1.0).astype(f32)

    def listed(s, side):
        return META[side, 2:3, span(s * block, block)] * present(side)

    def split(values, slot):
        cols = span(slot * half, half)
        high = values.astype(bf16)
        UH[0:rows2, cols] = high
        UH[rows2 : 2 * rows2, cols] = (values - high.astype(f32)).astype(bf16)

    factor = 1.0 / (SCALE * (rows * nmem - 1))

    def multiply(s, first_row, first_block, count):
        cols = span(first_block * block, count * block) if isinstance(first_block, int) else pl.ds(
            pl.multiple_of(first_block * block, block), count * block
        )
        at = pl.ds(pl.multiple_of(first_row * block, block), count * block)
        full = jnp.dot(UH[:, cols], CH[s, at, :], preferred_element_type=f32)
        low = jnp.dot(UH[0:rows2, cols], CL[s, at, :], preferred_element_type=f32)
        return (full[0:rows2] + full[rows2:] + low) * factor

    def own_product(s):
        if s == 0:
            return multiply(0, 2, 2, 2)
        cols = slice(2 * block, 3 * block)
        at = slice(3 * block, 4 * block)
        turned = (((1,), (1,)), ((), ()))
        full = lax.dot_general(UH[:, cols], CH[0, at, :], turned, preferred_element_type=f32)
        low = lax.dot_general(UH[0:rows2, cols], CL[0, at, :], turned, preferred_element_type=f32)
        return multiply(1, 2, 3, 1) + (full[0:rows2] + full[rows2:] + low) * factor

    def cross_product(side):
        return multiply(1 - side, 4 * side, 1 + 3 * side, 1)

    def side_product(side):
        return multiply(side, 3 * side, 4 * side, 2)

    def noise(s):
        return oerr[:, pl.ds(pl.multiple_of(c * half + s * block, block), block)]

    def wait_anomalies(side):
        remote(X.at[1], X.at[2 * side], f_send.at[0, 0], f_recv.at[1 - side], partner).wait_recv()

    def couple_cross(side):
        s, w = cross_pair(side)
        couple(s, w, listed(s, side))

    def couple_side(side):
        couple(*next_pair(side), present(side))
        s, w = outer_pair(side)
        couple(s, w, listed(s, side))

    turn(1)
    for s, w in ((0, 2), (0, 3), (1, 3)):
        couple(s, w)
    u_in[2].wait_recv()
    split(U[1], 1)
    for s in range(2):
        cols = slice(s * block, (s + 1) * block)
        V[1, :, cols] = U[1, :, cols] * noise(s) + own_product(s)
    remote(innov.at[:, own_half], U.at[2 * on_side, partner_rows, :], u_send.at[0], u_recv.at[1 - on_side], partner).wait_recv()
    split(U[2 * on_side], 2 * on_side)
    wait_anomalies(on_side)
    turn(2 * on_side)
    couple_cross(on_side)
    couple_side(on_side)
    V[1, :, span((1 - on_side) * block, block)] += cross_product(on_side)
    V[1, :, span(on_side * block, block)] += side_product(on_side)
    widen(2)
    remote(innov.at[:, own_half], U.at[2 * off_side, partner_rows, :], u_send.at[0], u_recv.at[1 - off_side], partner).wait_recv()
    u_in[3].wait_recv()
    split(U[2 * off_side], 2 * off_side)
    wait_anomalies(off_side)
    turn(2 * off_side)

    v_out = []

    def send_image(s, part):
        cols = span(s * block, block)
        v_out.append(remote(V.at[1, :, cols], V.at[2, :, cols], v_send.at[0, part], v_recv.at[0, part], left))
        v_out.append(remote(V.at[1, :, cols], V.at[0, :, cols], v_send.at[1, part], v_recv.at[1, part], right))
        v_out[-2].start()
        v_out[-1].start()

    couple_cross(off_side)
    V[1, :, span((1 - off_side) * block, block)] += cross_product(off_side)
    send_image(1 - off_side, 0)
    couple_side(off_side)
    V[1, :, span(off_side * block, block)] += side_product(off_side)
    send_image(off_side, 1)

    u1_copy = [pltpu.make_async_copy(V.at[1, core_rows, :], u1_out.at[:, own_half], o_sem.at[0])]
    u1_copy[0].start()

    def lane_sums(d, value):
        total = value[:, 0:LANES]
        for k in range(1, half // LANES):
            total = total + value[:, k * LANES : (k + 1) * LANES]
        for h in range(2):
            PP[(4 * h + d) * rows : (4 * h + d + 1) * rows, :] = total[h * rows : (h + 1) * rows]

    def wait_image(side):
        for part in range(2):
            s = c if part == 0 else 1 - c
            cols = span(s * block, block)
            remote(
                V.at[1, :, cols], V.at[2 * side, :, cols], v_send.at[0, part], v_recv.at[1 - side, part], partner
            ).wait_recv()
        split(V[2 * side], 2 * side)

    split(V[1], 1)
    for s in range(2):
        cols = slice(s * block, (s + 1) * block)
        W2[:, cols] = V[1, :, cols] * noise(s) + own_product(s)
    lane_sums(0, U[1] * U[1])
    lane_sums(1, U[1] * V[1])
    lane_sums(2, V[1] * V[1])
    wait_image(on_side)
    W2[:, span((1 - on_side) * block, block)] += cross_product(on_side)
    W2[:, span(on_side * block, block)] += side_product(on_side)
    widen(3)
    wait_image(off_side)
    W2[:, span((1 - off_side) * block, block)] += cross_product(off_side)
    W2[:, span(off_side * block, block)] += side_product(off_side)

    lane_sums(3, V[1] * W2[...])
    row = jnp.sum(PP[...].T, axis=0, keepdims=True)
    SB[0:1, :] = row[:, 0 : 4 * rows]
    SB[1:2, :] = row[:, 4 * rows :]
    e_copy = remote(SB.at[pl.ds(1 - c, 1), :], SR, e_send, e_recv, partner)
    e_copy.start()
    w_copy = remote(W2.at[partner_rows, :], W3, w_send, w_recv, partner)
    w_copy.start()
    e_copy.wait_recv()
    G[pl.ds(o, 1), :] = SB[pl.ds(c, 1), :] + SR[...]
    mine = G.at[pl.ds(o, 1), :]
    offsets = [(dz, dx) for dz in range(nz) for dx in range(nx) if dz or dx]
    offsets.sort(key=lambda d: -(min(d[0], nz - d[0]) + min(d[1], nx - d[1])))
    for dz, dx in offsets:
        remote(mine, mine, g_send, g_recv, peer(dz, dx)).start()
    u1_copy.append(
        pltpu.make_async_copy(V.at[2 - 2 * c, core_rows, :], u1_out.at[:, other_half], o_sem.at[1])
    )
    u2_copy = [
        pltpu.make_async_copy(W2.at[core_rows, :], u2_out.at[:, own_half], o_sem.at[2]),
        pltpu.make_async_copy(W3, u2_out.at[:, other_half], o_sem.at[3]),
    ]
    u1_copy[1].start()
    u2_copy[0].start()
    w_copy.wait_recv()
    u2_copy[1].start()
    rest = G.at[0 : nobs - 1, :]
    remote(rest, rest, g_send, g_recv, partner).wait_recv()
    sums = jnp.sum(G[...], axis=0, keepdims=True)

    norm = sums[:, 0:rows]
    cross = sums[:, rows : 2 * rows]
    image = sums[:, 2 * rows : 3 * rows]
    size = norm / cross
    norm_next = size * size * image - norm
    more = 1.0 + norm_next / (norm + EPSILON)
    curve = (more * cross - 2.0 * size * image) * more + size * size * sums[:, 3 * rows :]
    size_next = norm_next / curve
    place = lax.broadcasted_iota(jnp.int32, (LANES, rows), 0)
    table = jnp.where(place == 0, size + size_next * more, size * size_next)
    table = jnp.concatenate([table, jnp.zeros((LANES, LANES - rows), f32)], axis=1)
    c_out[...] = table.T[0:rows, :]

    for copy in [meta_copy] + a_out + relays + f_out + u_out + v_out + [e_copy, w_copy]:
        copy.wait_send()
    remote(rest, rest, g_send, g_recv, partner).wait_send()
    for copy in u1_copy + u2_copy:
        copy.wait()


def combine(start, image, again, factors, x_out, r_out):
    linear, square = factors[:, 0:1], factors[:, 1:2]
    x_out[...] = linear * start[...] - square * image[...]
    r_out[...] = start[...] - linear * image[...] + square * again[...]


def body(anomalies, innovations, obs_error, positions, pair_far, block, nx):
    f32, bf16 = jnp.float32, jnp.bfloat16
    rows, width = anomalies.shape
    nobs, nmem = lax.axis_size("obs"), lax.axis_size("mem")
    half, rows2, members = 2 * block, 2 * rows, rows * nmem
    vmem = pl.BlockSpec(memory_space=pltpu.VMEM)
    whole = pl.BlockSpec(memory_space=pl.ANY)
    dma = pltpu.SemaphoreType.DMA
    scratch = [
        pltpu.VMEM((3, members, half), bf16),
        pltpu.VMEM((3 * half, members), bf16),
        pltpu.VMEM((3, rows2, half), f32),
        pltpu.VMEM((3, rows2, half), f32),
        pltpu.VMEM((2 * rows2, 3 * half), bf16),
        pltpu.VMEM((2, 5 * block, block), bf16),
        pltpu.VMEM((2, 5 * block, block), bf16),
        pltpu.VMEM((2, 5 * block, block), f32),
        pltpu.VMEM((2, 3 * half, LANES), f32),
        pltpu.VMEM((3, 8, half), f32),
        pltpu.VMEM((8 * rows, LANES), f32),
        pltpu.VMEM((rows2, half), f32),
        pltpu.VMEM((rows, half), f32),
        pltpu.VMEM((2, 4 * rows), f32),
        pltpu.VMEM((1, 4 * rows), f32),
        pltpu.VMEM((nobs, 4 * rows), f32),
        dma((7,)), dma((7,)),
        dma((2, 8)), dma((2,)),
        dma((4,)), dma((4,)),
        dma, dma,
        dma((2, 2)), dma((2, 2)),
        dma, dma,
        dma, dma,
        dma, dma,
        pltpu.SemaphoreType.REGULAR((4,)),
        dma((4,)),
    ]
    image, again, factors = pl.pallas_call(
        functools.partial(kernel, block, nobs, nmem, nx),
        out_shape=[jax.ShapeDtypeStruct((rows, width), f32)] * 2 + [jax.ShapeDtypeStruct((rows, LANES), f32)],
        in_specs=[vmem] * 4 + [pl.BlockSpec(memory_space=pltpu.SMEM)],
        out_specs=[whole, whole, vmem],
        scratch_shapes=scratch,
        compiler_params=pltpu.CompilerParams(
            collective_id=0, has_side_effects=True, vmem_limit_bytes=56 * 1024 * 1024
        ),
        name="filter_steps",
    )(anomalies, innovations, obs_error[None, :], positions, pair_far)
    return tuple(
        pl.pallas_call(
            combine,
            out_shape=[jax.ShapeDtypeStruct((rows, width), f32)] * 2,
            in_specs=[vmem] * 4,
            out_specs=[vmem] * 2,
            name="combine",
        )(innovations, image, again, factors)
    )


def solution(mesh, block=B, nx=NX):
    in_specs = (P("mem", "obs"), P("mem", "obs"), P("obs"), P(None, "obs"), P("obs"))
    out_specs = (P("mem", "obs"), P("mem", "obs"))
    return jax.shard_map(
        functools.partial(body, block=block, nx=nx),
        mesh=mesh,
        in_specs=in_specs,
        out_specs=out_specs,
        check_vma=False,
    )
```

```python
import functools
import math

import jax
import jax.numpy as jnp
from jax import lax
from jax.experimental import pallas as pl
from jax.experimental.pallas import tpu as pltpu
from jax.sharding import PartitionSpec as P

B = 512
NX = 4
EPSILON = 1e-06
ROOT2 = math.sqrt(2.0)
SCALE = 48.0 * ROOT2
MESH = pl.DeviceIdType.MESH
LANES = 128
CHUNK = 128


def remote(src, dst, send, recv, device):
    return pltpu.make_async_remote_copy(
        src_ref=src, dst_ref=dst, send_sem=send, recv_sem=recv, device_id=device, device_id_type=MESH
    )


def kernel(
    block, nobs, nmem, nx,
    anom, innov, oerr, places, far, u1_out, u2_out, c_out,
    X, XT, U, V, UH, CH, CL, TP, PI, META, PP, W2, W3, SB, SR, G,
    a_send, a_recv, f_send, f_recv, u_send, u_recv, m_send, m_recv, v_send, v_recv, w_send, w_recv,
    e_send, e_recv, g_send, g_recv, reach, o_sem,
):
    f32, bf16 = jnp.float32, jnp.bfloat16
    half = 2 * block
    rows = anom.shape[0]
    rows2 = 2 * rows
    nz = nobs // nx
    o = lax.axis_index("obs")
    mm = lax.axis_index("mem")
    c = lax.rem(mm, 2)
    y2 = mm - c
    up = lax.rem(y2 + 2, nmem)
    down = lax.rem(y2 + nmem - 2, nmem)
    across_y = lax.rem(y2 + nmem // 2, nmem)
    pm = y2 + 1 - c
    z = lax.div(o, nx)
    x = lax.rem(o, nx)
    left = (lax.rem(o + nobs - 1 + c, nobs), pm)
    right = (lax.rem(o + c, nobs), pm)
    partner = (o, pm)
    far_to = (lax.rem(o + nobs + 1 - 2 * c, nobs), mm)
    far_from = (lax.rem(o + nobs - 1 + 2 * c, nobs), mm)
    off_chip = (lax.rem(o + nobs - 1 + 2 * c, nobs), pm)

    def peer(dz, dx):
        return (lax.rem(z + dz + nz, nz) * nx + lax.rem(x + dx + nx, nx), mm)

    barrier = pltpu.get_barrier_semaphore()
    near = [partner, left, right, far_to, far_from]
    near += [(o, y + k) for y in (up, down) for k in range(2)]
    near += [peer(0, dx) for dx in range(1, nx)]
    near += [peer(dz, 0) for dz in sorted({1, nz - 1})]
    for device in near:
        pl.semaphore_signal(barrier, inc=1, device_id=device, device_id_type=MESH)

    own_rows = pl.ds(pl.multiple_of(mm * rows, rows), rows)
    core_rows = pl.ds(pl.multiple_of(c * rows, rows), rows)
    partner_rows = pl.ds(pl.multiple_of((1 - c) * rows, rows), rows)
    own_half = pl.ds(pl.multiple_of(c * half, half), half)
    other_half = pl.ds(pl.multiple_of((1 - c) * half, half), half)
    pf = places[...].astype(f32) * ROOT2
    for h in range(2):
        flags = jnp.concatenate(
            [jnp.full((1, block), far[2 * h + b].astype(f32), f32) for b in range(2)], axis=1
        )
        META[1 - c + h] = jnp.concatenate(
            [pf[:, h * half : (h + 1) * half], flags, jnp.zeros((5, half), f32)], axis=0
        )
    X[1, own_rows, :] = anom[:, own_half]
    off_side, on_side = c, 1 - c

    def span(start, size):
        return pl.ds(start if isinstance(start, int) else pl.multiple_of(start, size), size)

    def columns(slot):
        for k in range(half // LANES):
            for axis in range(2):
                line = META[slot, axis : axis + 1, k * LANES : (k + 1) * LANES]
                PI[axis, span(slot * half + k * LANES, LANES), :] = jnp.broadcast_to(line, (LANES, LANES)).T

    def taper(s, w, close):
        cols = span(s * block, block)
        shift = (w - 2 - s) * ROOT2 if isinstance(w, int) else (w - 2 - s).astype(f32) * ROOT2
        along = META[1, 0:1, cols] - shift
        across = META[1, 1:2, cols]
        times = block // LANES

        def step(k, carry):
            theirs = span(w * block + k * CHUNK, CHUNK)
            g = jnp.concatenate([PI[0, theirs, :]] * times, axis=1) - along
            h = jnp.concatenate([PI[1, theirs, :]] * times, axis=1) - across
            square = g * g + h * h
            if close:
                square = jnp.maximum(square, 1e-30)
            inverse = lax.rsqrt(square)
            y = square * inverse
            rest = jnp.maximum(2.0 * ROOT2 - y, 0.0)
            rest = rest * rest
            value = (rest * rest) * ((y - inverse) + 2.0 * ROOT2)
            if close:
                inner = (-3.0 * y + 0.125 * SCALE) * y + 0.3125 * SCALE / ROOT2
                inner = (inner * y - (5.0 / 6.0) * SCALE) * square + SCALE
                value = jnp.maximum(value, inner)
            TP[s, span((w - s) * block + k * CHUNK, CHUNK), :] = value
            return carry

        lax.fori_loop(0, block // CHUNK, step, 0)

    def cross_pair(side):
        return 1 - side, 1 + 3 * side

    def next_pair(side):
        return side, 1 + 3 * side

    def outer_pair(side):
        return side, 5 * side

    columns(1)
    taper(0, 2, True)
    pl.semaphore_wait(barrier, len(near))

    steps = [step for step in (1, 2, 4, 8) if 2 * step <= nz]

    def tell(k):
        for dz in sorted({steps[k], nz - steps[k]}):
            pl.semaphore_signal(reach.at[k], inc=1, device_id=peer(dz, 0), device_id_type=MESH)

    def hear(k):
        pl.semaphore_wait(reach.at[k], len({steps[k], nz - steps[k]}))

    def widen(k):
        if k < len(steps):
            hear(k)
            if k + 1 < len(steps):
                tell(k + 1)

    meta_copy = remote(META.at[1], META.at[2 - 2 * c], m_send, m_recv, off_chip)
    meta_copy.start()
    meta_back = remote(META.at[1], META.at[2 * c], m_send, m_recv, off_chip)

    def half_of(core):
        return pl.ds(pl.multiple_of(core * half, half), half)

    def rows_of(member):
        return pl.ds(pl.multiple_of(member * rows, rows), rows)

    a_out = []
    for way, slot in ((up + c * (down - up), 1 + 3 * c), (down + c * (up - down), 3 - c)):
        for core in range(2):
            k = lax.rem(c + core, 2)
            copy = remote(
                anom.at[:, half_of(k)], X.at[1, own_rows, :], a_send.at[len(a_out) + 1], a_recv.at[slot], (o, way + k)
            )
            a_out.append(copy)
    a_out.append(remote(anom.at[:, other_half], X.at[1, own_rows, :], a_send.at[0], a_recv.at[0], partner))
    for copy in a_out:
        copy.start()

    u_out = [
        remote(innov.at[:, own_half], U.at[2, core_rows, :], u_send.at[0], u_recv.at[0], left),
        remote(innov.at[:, own_half], U.at[0, core_rows, :], u_send.at[1], u_recv.at[1], right),
        remote(innov.at[:, other_half], U.at[1, core_rows, :], u_send.at[2], u_recv.at[2], partner),
        remote(innov.at[:, other_half], U.at[2 * c, core_rows, :], u_send.at[3], u_recv.at[3], far_to),
    ]
    u_in = [
        remote(innov.at[:, own_half], U.at[2, partner_rows, :], u_send.at[0], u_recv.at[0], left),
        remote(innov.at[:, own_half], U.at[0, partner_rows, :], u_send.at[1], u_recv.at[1], right),
        remote(innov.at[:, other_half], U.at[1, partner_rows, :], u_send.at[2], u_recv.at[2], partner),
        remote(innov.at[:, other_half], U.at[2 * c, core_rows, :], u_send.at[3], u_recv.at[3], far_to),
    ]

    sources = [mm, pm, down, down + 1, up, up + 1, across_y, across_y + 1]
    f_out, relays = [], []

    def arrived(k):
        piece = rows_of(sources[k])
        remote(anom.at[:, own_half], X.at[1, piece, :], a_send.at[k - 1], a_recv.at[k - 1], partner).wait_recv()

    def forward(k):
        piece = rows_of(sources[k])
        if k > 0:
            arrived(k)
        if k == 2:
            relays.append(remote(X.at[1, piece, :], X.at[1, piece, :], a_send.at[5], a_recv.at[5], (o, up + c)))
            relays[-1].start()
        if k == 5:
            relays.append(remote(X.at[1, piece, :], X.at[1, piece, :], a_send.at[6], a_recv.at[6], (o, down + c)))
            relays[-1].start()
        one = remote(X.at[1, piece, :], X.at[2, piece, :], f_send.at[0, k], f_recv.at[0], left)
        two = remote(X.at[1, piece, :], X.at[0, piece, :], f_send.at[1, k], f_recv.at[1], right)
        one.start()
        two.start()
        f_out.extend([one, two])

    forward(0)
    for copy in u_out:
        copy.start()
    tell(0)
    for h in range(2):
        U[1 - c + h, core_rows, :] = innov[:, h * half : (h + 1) * half]

    columns(2 * on_side)
    taper(0, 3, True)
    forward(1)
    taper(1, 3, True)
    taper(*next_pair(on_side), True)
    forward(2)
    taper(*cross_pair(on_side), False)
    forward(5)
    taper(*outer_pair(on_side), False)
    forward(3)
    forward(4)
    widen(0)
    meta_back.wait_recv()
    columns(2 * off_side)
    taper(*cross_pair(off_side), False)
    taper(*next_pair(off_side), True)
    forward(6)
    taper(*outer_pair(off_side), False)
    forward(7)
    widen(1)

    def turn(slot):
        part = 2 * LANES
        for k in range(half // part):
            XT[span(slot * half + k * part, part), :] = X[slot, :, k * part : (k + 1) * part].T

    def couple(s, w, factor=None):
        at = span((w - s) * block, block)
        value = jnp.dot(
            XT[span(w * block, block), :], X[1, :, span(s * block, block)], preferred_element_type=f32
        ) * TP[s, at, :]
        if factor is not None:
            value = value * factor
        high = value.astype(bf16)
        CH[s, at, :] = high
        CL[s, at, :] = (value - high.astype(f32)).astype(bf16)

    def present(side):
        chain = 2 * o + c
        edge = jnp.where(side == 0, 0, 2 * nobs - 1)
        return jnp.where(chain == edge, 0.0, 1.0).astype(f32)

    def listed(s, side):
        return META[side, 2:3, span(s * block, block)] * present(side)

    def split(values, slot):
        cols = span(slot * half, half)
        high = values.astype(bf16)
        UH[0:rows2, cols] = high
        UH[rows2 : 2 * rows2, cols] = (values - high.astype(f32)).astype(bf16)

    factor = 1.0 / (SCALE * (rows * nmem - 1))

    def multiply(s, first_row, first_block, count):
        cols = span(first_block * block, count * block) if isinstance(first_block, int) else pl.ds(
            pl.multiple_of(first_block * block, block), count * block
        )
        at = pl.ds(pl.multiple_of(first_row * block, block), count * block)
        full = jnp.dot(UH[:, cols], CH[s, at, :], preferred_element_type=f32)
        low = jnp.dot(UH[0:rows2, cols], CL[s, at, :], preferred_element_type=f32)
        return (full[0:rows2] + full[rows2:] + low) * factor

    def own_product(s):
        if s == 0:
            return multiply(0, 2, 2, 2)
        cols = slice(2 * block, 3 * block)
        at = slice(3 * block, 4 * block)
        turned = (((1,), (1,)), ((), ()))
        full = lax.dot_general(UH[:, cols], CH[0, at, :], turned, preferred_element_type=f32)
        low = lax.dot_general(UH[0:rows2, cols], CL[0, at, :], turned, preferred_element_type=f32)
        return multiply(1, 2, 3, 1) + (full[0:rows2] + full[rows2:] + low) * factor

    def cross_product(side):
        return multiply(1 - side, 4 * side, 1 + 3 * side, 1)

    def side_product(side):
        return multiply(side, 3 * side, 4 * side, 2)

    def noise(s):
        return oerr[:, pl.ds(pl.multiple_of(c * half + s * block, block), block)]

    def wait_anomalies(side):
        remote(X.at[1], X.at[2 * side], f_send.at[0, 0], f_recv.at[1 - side], partner).wait_recv()

    def couple_cross(side):
        s, w = cross_pair(side)
        couple(s, w, listed(s, side))

    def couple_side(side):
        couple(*next_pair(side), present(side))
        s, w = outer_pair(side)
        couple(s, w, listed(s, side))

    turn(1)
    for s, w in ((0, 2), (0, 3), (1, 3)):
        couple(s, w)
    u_in[2].wait_recv()
    split(U[1], 1)
    for s in range(2):
        cols = slice(s * block, (s + 1) * block)
        V[1, :, cols] = U[1, :, cols] * noise(s) + own_product(s)
    remote(innov.at[:, own_half], U.at[2 * on_side, partner_rows, :], u_send.at[0], u_recv.at[1 - on_side], partner).wait_recv()
    split(U[2 * on_side], 2 * on_side)
    wait_anomalies(on_side)
    turn(2 * on_side)
    couple_cross(on_side)
    couple_side(on_side)
    V[1, :, span((1 - on_side) * block, block)] += cross_product(on_side)
    V[1, :, span(on_side * block, block)] += side_product(on_side)
    widen(2)
    remote(innov.at[:, own_half], U.at[2 * off_side, partner_rows, :], u_send.at[0], u_recv.at[1 - off_side], partner).wait_recv()
    u_in[3].wait_recv()
    split(U[2 * off_side], 2 * off_side)
    wait_anomalies(off_side)
    turn(2 * off_side)

    v_out = []

    def send_image(s, part):
        cols = span(s * block, block)
        v_out.append(remote(V.at[1, :, cols], V.at[2, :, cols], v_send.at[0, part], v_recv.at[0, part], left))
        v_out.append(remote(V.at[1, :, cols], V.at[0, :, cols], v_send.at[1, part], v_recv.at[1, part], right))
        v_out[-2].start()
        v_out[-1].start()

    couple_cross(off_side)
    V[1, :, span((1 - off_side) * block, block)] += cross_product(off_side)
    send_image(1 - off_side, 0)
    couple_side(off_side)
    V[1, :, span(off_side * block, block)] += side_product(off_side)
    send_image(off_side, 1)

    u1_copy = [pltpu.make_async_copy(V.at[1, core_rows, :], u1_out.at[:, own_half], o_sem.at[0])]
    u1_copy[0].start()

    def lane_sums(d, value):
        total = value[:, 0:LANES]
        for k in range(1, half // LANES):
            total = total + value[:, k * LANES : (k + 1) * LANES]
        for h in range(2):
            PP[(4 * h + d) * rows : (4 * h + d + 1) * rows, :] = total[h * rows : (h + 1) * rows]

    def wait_image(side):
        for part in range(2):
            s = c if part == 0 else 1 - c
            cols = span(s * block, block)
            remote(
                V.at[1, :, cols], V.at[2 * side, :, cols], v_send.at[0, part], v_recv.at[1 - side, part], partner
            ).wait_recv()
        split(V[2 * side], 2 * side)

    split(V[1], 1)
    for s in range(2):
        cols = slice(s * block, (s + 1) * block)
        W2[:, cols] = V[1, :, cols] * noise(s) + own_product(s)
    lane_sums(0, U[1] * U[1])
    lane_sums(1, U[1] * V[1])
    lane_sums(2, V[1] * V[1])
    wait_image(on_side)
    W2[:, span((1 - on_side) * block, block)] += cross_product(on_side)
    W2[:, span(on_side * block, block)] += side_product(on_side)
    widen(3)
    wait_image(off_side)
    W2[:, span((1 - off_side) * block, block)] += cross_product(off_side)
    W2[:, span(off_side * block, block)] += side_product(off_side)

    lane_sums(3, V[1] * W2[...])
    row = jnp.sum(PP[...].T, axis=0, keepdims=True)
    SB[0:1, :] = row[:, 0 : 4 * rows]
    SB[1:2, :] = row[:, 4 * rows :]
    e_copy = remote(SB.at[pl.ds(1 - c, 1), :], SR, e_send, e_recv, partner)
    e_copy.start()
    w_copy = remote(W2.at[partner_rows, :], W3, w_send, w_recv, partner)
    w_copy.start()
    e_copy.wait_recv()
    G[pl.ds(o, 1), :] = SB[pl.ds(c, 1), :] + SR[...]
    mine = G.at[pl.ds(o, 1), :]
    offsets = [(dz, dx) for dz in range(nz) for dx in range(nx) if dz or dx]
    offsets.sort(key=lambda d: -(min(d[0], nz - d[0]) + min(d[1], nx - d[1])))
    for dz, dx in offsets:
        remote(mine, mine, g_send, g_recv, peer(dz, dx)).start()
    u1_copy.append(
        pltpu.make_async_copy(V.at[2 - 2 * c, core_rows, :], u1_out.at[:, other_half], o_sem.at[1])
    )
    u2_copy = [
        pltpu.make_async_copy(W2.at[core_rows, :], u2_out.at[:, own_half], o_sem.at[2]),
        pltpu.make_async_copy(W3, u2_out.at[:, other_half], o_sem.at[3]),
    ]
    u1_copy[1].start()
    u2_copy[0].start()
    w_copy.wait_recv()
    u2_copy[1].start()
    rest = G.at[0 : nobs - 1, :]
    remote(rest, rest, g_send, g_recv, partner).wait_recv()
    sums = jnp.sum(G[...], axis=0, keepdims=True)

    norm = sums[:, 0:rows]
    cross = sums[:, rows : 2 * rows]
    image = sums[:, 2 * rows : 3 * rows]
    size = norm / cross
    norm_next = size * size * image - norm
    more = 1.0 + norm_next / (norm + EPSILON)
    curve = (more * cross - 2.0 * size * image) * more + size * size * sums[:, 3 * rows :]
    size_next = norm_next / curve
    place = lax.broadcasted_iota(jnp.int32, (LANES, rows), 0)
    table = jnp.where(place == 0, size + size_next * more, size * size_next)
    table = jnp.concatenate([table, jnp.zeros((LANES, LANES - rows), f32)], axis=1)
    c_out[...] = table.T[0:rows, :]

    for copy in [meta_copy] + a_out + relays + f_out + u_out + v_out + [e_copy, w_copy]:
        copy.wait_send()
    remote(rest, rest, g_send, g_recv, partner).wait_send()
    for copy in u1_copy + u2_copy:
        copy.wait()


def combine(start, image, again, factors, x_out, r_out):
    linear, square = factors[:, 0:1], factors[:, 1:2]
    x_out[...] = linear * start[...] - square * image[...]
    r_out[...] = start[...] - linear * image[...] + square * again[...]


def body(anomalies, innovations, obs_error, positions, pair_far, block, nx):
    f32, bf16 = jnp.float32, jnp.bfloat16
    rows, width = anomalies.shape
    nobs, nmem = lax.axis_size("obs"), lax.axis_size("mem")
    half, rows2, members = 2 * block, 2 * rows, rows * nmem
    vmem = pl.BlockSpec(memory_space=pltpu.VMEM)
    whole = pl.BlockSpec(memory_space=pl.ANY)
    dma = pltpu.SemaphoreType.DMA
    scratch = [
        pltpu.VMEM((3, members, half), bf16),
        pltpu.VMEM((3 * half, members), bf16),
        pltpu.VMEM((3, rows2, half), f32),
        pltpu.VMEM((3, rows2, half), f32),
        pltpu.VMEM((2 * rows2, 3 * half), bf16),
        pltpu.VMEM((2, 5 * block, block), bf16),
        pltpu.VMEM((2, 5 * block, block), bf16),
        pltpu.VMEM((2, 5 * block, block), f32),
        pltpu.VMEM((2, 3 * half, LANES), f32),
        pltpu.VMEM((3, 8, half), f32),
        pltpu.VMEM((8 * rows, LANES), f32),
        pltpu.VMEM((rows2, half), f32),
        pltpu.VMEM((rows, half), f32),
        pltpu.VMEM((2, 4 * rows), f32),
        pltpu.VMEM((1, 4 * rows), f32),
        pltpu.VMEM((nobs, 4 * rows), f32),
        dma((7,)), dma((7,)),
        dma((2, 8)), dma((2,)),
        dma((4,)), dma((4,)),
        dma, dma,
        dma((2, 2)), dma((2, 2)),
        dma, dma,
        dma, dma,
        dma, dma,
        pltpu.SemaphoreType.REGULAR((4,)),
        dma((4,)),
    ]
    image, again, factors = pl.pallas_call(
        functools.partial(kernel, block, nobs, nmem, nx),
        out_shape=[jax.ShapeDtypeStruct((rows, width), f32)] * 2 + [jax.ShapeDtypeStruct((rows, LANES), f32)],
        in_specs=[vmem] * 4 + [pl.BlockSpec(memory_space=pltpu.SMEM)],
        out_specs=[whole, whole, vmem],
        scratch_shapes=scratch,
        compiler_params=pltpu.CompilerParams(
            collective_id=0, has_side_effects=True, vmem_limit_bytes=56 * 1024 * 1024
        ),
        name="filter_steps",
    )(anomalies, innovations, obs_error[None, :], positions, pair_far)
    return tuple(
        pl.pallas_call(
            combine,
            out_shape=[jax.ShapeDtypeStruct((rows, width), f32)] * 2,
            in_specs=[vmem] * 4,
            out_specs=[vmem] * 2,
            name="combine",
        )(innovations, image, again, factors)
    )


def solution(mesh, block=B, nx=NX):
    in_specs = (P("mem", "obs"), P("mem", "obs"), P("obs"), P(None, "obs"), P("obs"))
    out_specs = (P("mem", "obs"), P("mem", "obs"))
    return jax.shard_map(
        functools.partial(body, block=block, nx=nx),
        mesh=mesh,
        in_specs=in_specs,
        out_specs=out_specs,
        check_vma=False,
    )
```
